512 devices in a mesh: sup: 64 (over z, y), cls: 8 (over x, core).
Axes of the slice: x: 4, y: 4, z: 16, core: 2. Of those that a mesh axis runs over, the one named last changes fastest.
Arguments:
- support_feats: bfloat16 [2048, 8192], P('sup', 'cls'), may hold values from -6 to 6
- target_feats: bfloat16 [512, 8192], P('sup', 'cls'), may hold values from -6 to 6
- scales: bfloat16 [2048], replicated, may hold values from 0.5 to 2
- soft_labels: float32 [2048, 21504], P('sup', 'cls'), may hold values from -6 to 6
- target_labels: int32 [512], P('sup'), may hold values from 0 to 21503
Outputs:
- predictions: bfloat16 [512, 21504], P('sup', 'cls')
- hypergrad: float32 [2048, 21504], P('sup', 'cls')
The draws below stay inside these ranges and needn't reach their ends.
All inputs are finite; a program needn't handle non-finite values.
Results may differ from the reference program's by a relative error of at most 0.017.
Values may be sent and summed in bfloat16 or wider, within the bound.
A program may use at most 64 MiB of HBM per device.

```python
import math
import jax
import jax.numpy as jnp
from jax import lax

F = 8192
ITERS = 2
C = 21504
NS = 2048
NT = 512


def touch_ends(array, rng, low, top_value):
    index_at = [jax.random.randint(jax.random.fold_in(rng, axis), (), 0, length) for axis, length in enumerate(array.shape)]
    main_axis = array.shape.index(max(array.shape))
    next_to = index_at[:main_axis] + [(index_at[main_axis] + 1) % array.shape[main_axis]] + index_at[main_axis + 1:]
    return array.at[tuple(index_at)].set(low).at[tuple(next_to)].set(top_value)


def level_of(rng, dims, shards, least, high):
    level = 1.0
    for position, shards_of in shards:
        steps = jax.random.uniform(jax.random.fold_in(jax.random.fold_in(rng, 6), position), (shards_of,), jnp.float32, least / len(shards), high / len(shards))
        level = level * jnp.repeat(jnp.exp(steps), dims[position] // shards_of).reshape((-1,) + (1,) * (len(dims) - 1 - position))
    return level


def noise(rng, extent, deviation, limit, cuts=(), kind=jnp.bfloat16):
    values = deviation * jax.random.normal(rng, extent, jnp.float32)
    if cuts:
        values = values * level_of(rng, extent, cuts, -0.22, 0.18)
    return jnp.clip(values, -limit, limit).astype(kind)


def setup_inputs(seed: int = 0) -> dict:
    key_of = jax.random.split(jax.random.key(seed), 6)
    return {
        "support_feats": noise(key_of[0], (NS, F), 1.0, 6.0, ((0, 64), (1, 8))),
        "target_feats": noise(key_of[1], (NT, F), 1.0, 6.0, ((0, 64), (1, 8))),
        "scales": jnp.clip(jnp.exp(jax.random.uniform(key_of[2], (NS,), jnp.float32, math.log(0.5), math.log(2.0))), 0.5, 2.0).astype(jnp.bfloat16),
        "soft_labels": noise(key_of[3], (NS, C), 1.0, 6.0, ((0, 64), (1, 8)), jnp.float32),
        "target_labels": touch_ends(jax.random.randint(key_of[4], (NT,), 0, C), jax.random.fold_in(key_of[4], 1), 0, C - 1).astype(jnp.int32),
    }


RIDGE = 0.05
LABEL_SCALE = 16.0


def solve(kernel, rhs):
    result = jnp.zeros_like(rhs)
    resid = rhs
    direction = rhs
    norm_now = jnp.sum(resid * resid, axis=0)
    for step in range(ITERS):
        image = jnp.dot(kernel, direction.astype(jnp.bfloat16), preferred_element_type=jnp.float32)
        curve = jnp.sum(direction * image, axis=0)
        step_size = norm_now / curve
        result = result + step_size * direction
        resid = resid - step_size * image
        norm_next = jnp.sum(resid * resid, axis=0)
        direction = resid + (norm_next / norm_now) * direction
        norm_now = norm_next
    return result


def reference(support_feats, target_feats, scales, soft_labels, target_labels):
    scale_vec = scales.astype(jnp.float32)
    gram = jnp.dot(support_feats, support_feats.T, preferred_element_type=jnp.float32)
    support_kernel = (gram * (scale_vec[:, None] * scale_vec[None, :]) / F
                      + RIDGE * jnp.eye(NS, dtype=jnp.float32)).astype(jnp.bfloat16)
    alpha = solve(support_kernel, soft_labels)
    alpha_low = alpha.astype(jnp.bfloat16)
    cross_gram = jnp.dot(target_feats, support_feats.T, preferred_element_type=jnp.float32)
    cross_kernel = (cross_gram * scale_vec[None, :] / F).astype(jnp.bfloat16)
    predicted = jnp.dot(cross_kernel, alpha_low, preferred_element_type=jnp.float32)
    classes = jnp.arange(C, dtype=jnp.int32)
    onehot = (target_labels[:, None] == classes[None, :]).astype(jnp.float32)
    misfit = (predicted - LABEL_SCALE * onehot).astype(jnp.bfloat16)
    rhs = lax.dot_general(cross_kernel, misfit, (((0,), (0,)), ((), ())),
                          preferred_element_type=jnp.float32)
    hypergrad = solve(support_kernel, rhs)
    return predicted.astype(jnp.bfloat16), hypergrad
```

```python
import functools

import jax
import jax.numpy as jnp
from jax import lax
from jax.experimental import pallas as pl
from jax.experimental.pallas import tpu as pltpu
from jax.sharding import PartitionSpec as P

MESH = pl.DeviceIdType.MESH
F = 8192
RIDGE = 0.05
LABEL_SCALE = 16.0

NZ, NY, NX = 16, 4, 4
NSUP = NZ * NY
ROWS = 32
TROWS = 8
LANES = 128
BLOCKS = 21
PIECE = LANES + NY * TROWS
HALF = PIECE // 2
SENT = ROWS + 1
CELL = 40
F32 = jnp.float32
BF16 = jnp.bfloat16


def place():
    sup = lax.axis_index("sup")
    cls = lax.axis_index("cls")
    return sup // NY, sup % NY, cls // 2, cls % 2


def device(z, y, x, core):
    return {"sup": z * NY + y, "cls": x * 2 + core}


def signal(sem, dev):
    pl.semaphore_signal(sem, inc=1, device_id=dev, device_id_type=MESH)


def send(src, dst, send_sem, recv_sem, dev):
    pltpu.make_async_remote_copy(
        src_ref=src, dst_ref=dst, send_sem=send_sem, recv_sem=recv_sem, device_id=dev, device_id_type=MESH
    ).start()


def arrive(ref, sem):
    pltpu.make_async_copy(ref, ref, sem).wait()


def gram_kernel(feats, targets, scales, piece, jbuf, ibuf, tbuf, part, rbuf, zs, zr, ys, yr, ts, tr, xs, xr):
    z, y, x, core = place()
    up, down = (z + 1) % NZ, (z + NZ - 1) % NZ

    jbuf[z] = feats[...]
    ibuf[y] = feats[...]
    tfeats = targets[...].astype(F32)
    tbuf[y] = jnp.concatenate([tfeats, jnp.zeros_like(tfeats)], axis=0).astype(BF16)

    barrier = pltpu.get_barrier_semaphore()
    signal(barrier, device(up, y, x, core))
    signal(barrier, device(down, y, x, core))
    for k in range(1, NY):
        signal(barrier, device(z, (y + k) % NY, x, core))

    @pl.when(core == 0)
    def _():
        signal(barrier, device(z, y, x, 1))
        for k in range(1, NX):
            signal(barrier, device(z, y, (x + k) % NX, 0))
            signal(barrier, device(z, y, (x + k) % NX, 1))

    pl.semaphore_wait(barrier, 2 + NY - 1 + NX - 1 + core)

    def round_z(k):
        right, left = jbuf.at[(z + NZ - k) % NZ], jbuf.at[(z + k) % NZ]
        if k == NZ // 2 - 1:
            right, left = right.at[pl.ds(0, ROWS // 2)], left.at[pl.ds(ROWS // 2, ROWS // 2)]
        send(right, right, zs.at[0, k], zr.at[0, k], device(up, y, x, core))
        send(left, left, zs.at[1, k], zr.at[1, k], device(down, y, x, core))

    def wait_z(k):
        ref = jbuf.at[z]
        if k == NZ // 2 - 1:
            ref = ref.at[pl.ds(0, ROWS // 2)]
        arrive(ref, zr.at[0, k])
        arrive(ref, zr.at[1, k])

    round_z(0)
    for k in range(1, NY):
        dev = device(z, (y + k) % NY, x, core)
        send(ibuf.at[y], ibuf.at[y], ys.at[k - 1], yr.at[k - 1], dev)
        send(tbuf.at[y], tbuf.at[y], ts.at[k - 1], tr.at[k - 1], dev)
    for k in range(1, NZ // 2):
        wait_z(k - 1)
        round_z(k)
    for k in range(1, NY):
        arrive(ibuf.at[y], yr.at[k - 1])
        arrive(tbuf.at[y], tr.at[k - 1])
    wait_z(NZ // 2 - 1)

    cols = jbuf[...].reshape(NZ * ROWS, -1)
    over = (((1,), (1,)), ((), ()))
    gram = lax.dot_general(cols, ibuf[...].reshape(NY * ROWS, -1), over, preferred_element_type=F32)
    cross = lax.dot_general(tbuf[...].reshape(NY * 16, -1), cols, over, preferred_element_type=F32)
    cross = cross.reshape(NY, 16, NZ * ROWS)[:, :TROWS].reshape(NY * TROWS, NZ * ROWS)
    for k in range(NX):
        part[k, 0:LANES] = gram[k * LANES : (k + 1) * LANES]
        part[k, LANES:PIECE] = cross[:, k * LANES : (k + 1) * LANES]

    own = x * 2 + core
    for k in range(1, NX):
        to = (x + k) % NX
        send(part.at[to], rbuf.at[own], xs.at[k], xr, device(z, y, to, 0))

    @pl.when(core == 1)
    def _():
        send(part.at[x], rbuf.at[own], xs.at[0], xr, device(z, y, x, 0))
        arrive(part.at[x], xs.at[0])
        piece[...] = jnp.zeros_like(piece)

    @pl.when(core == 0)
    def _():
        rbuf[own] = part[x]
        arrive(rbuf.at[pl.ds(0, 2 * NX - 1)], xr)
        total = rbuf[0]
        for k in range(1, 2 * NX):
            total = total + rbuf[k]
        col_scale = scales[pl.ds(z, 1), :]
        lane = lax.broadcasted_iota(jnp.int32, (ROWS, LANES), 1)
        row = lax.broadcasted_iota(jnp.int32, (ROWS, LANES), 0)
        row_scales = []
        for a in range(4):
            zz = x * 4 + a
            picked = jnp.where(lane == y * ROWS + row, scales[pl.ds(zz, 1), :], 0.0)
            row_scale = jnp.sum(picked, axis=1, keepdims=True)
            row_scales.append(row_scale)
            diag = zz * LANES + y * ROWS + row == z * LANES + lane
            block = total[a * ROWS : (a + 1) * ROWS] * (row_scale * col_scale) / F
            piece[a * ROWS : (a + 1) * ROWS] = (block + jnp.where(diag, RIDGE, 0.0)).astype(BF16)
        row_scale = jnp.concatenate(row_scales, axis=0)
        same = lax.broadcasted_iota(jnp.int32, (LANES, LANES), 0) == lax.broadcasted_iota(jnp.int32, (LANES, LANES), 1)
        cross_scale = jnp.sum(jnp.where(same, row_scale, 0.0), axis=0, keepdims=True)
        piece[LANES:PIECE] = (total[LANES:PIECE] * cross_scale / F).astype(BF16)

    for k in range(1, NX):
        arrive(part.at[x], xs.at[k])
    for k in range(1, NY):
        arrive(ibuf.at[y], ys.at[k - 1])
        arrive(tbuf.at[y], ts.at[k - 1])
    for k in range(NZ // 2):
        ref = jbuf.at[z]
        if k == NZ // 2 - 1:
            ref = ref.at[pl.ds(0, ROWS // 2)]
        arrive(ref, zs.at[0, k])
        arrive(ref, zs.at[1, k])


def worker_sup(w):
    return (w * 32) // 21


def solve_kernel(
    piece, labels, classes, pred_out, hyper_out,
    kbuf, stage, bbuf, hbuf, pbuf, pn, bvec, vec, dvec, low, pred, hst,
    ls, lr, fs, fr, zs, zr, ds, dr, ws, wr, ps, pr, hs, hr,
):
    z, y, x, core = place()
    sup = z * NY + y
    up, down = (z + 1) % NZ, (z + NZ - 1) % NZ
    w = (sup * 21 + 31) // 32
    is_worker = (core == 0) & (worker_sup(w) == sup) & (w < 2 * BLOCKS)
    served = w // BLOCKS
    block = w % BLOCKS
    own_worker = is_worker & (served == 0)

    def to_worker(j):
        return worker_sup(core * BLOCKS + j)

    barrier = pltpu.get_barrier_semaphore()

    @pl.when(core == 0)
    def _():
        signal(barrier, device(up, y, x, 0))
        signal(barrier, device(down, y, x, 0))
        for k in range(1, NY):
            signal(barrier, device(z, (y + k) % NY, x, 0))
            signal(barrier, device(z, y, (x + k) % NX, 0))

    def greet_worker(j, c):
        to = to_worker(j)

        @pl.when((core == 1) | (to != sup))
        def _():
            signal(barrier, {"sup": to, "cls": x * 2})

        return c

    lax.fori_loop(0, BLOCKS, greet_worker, 0)

    @pl.when(is_worker)
    def _():
        def greet(s, c):
            @pl.when((served == 1) | (s != sup))
            def _():
                signal(barrier, {"sup": s, "cls": x * 2 + served})

            return c

        lax.fori_loop(0, NSUP, greet, 0)

    for j in range(BLOCKS):
        stage[j, 0:ROWS] = labels[:, j * LANES : (j + 1) * LANES]
        stage[j, ROWS:CELL] = classes[...]

    @pl.when(core == 0)
    def _():
        kbuf[z, y, x] = piece[...]

    peers = BLOCKS + jnp.where(core == 0, 2 + NY - 1 + NX - 1, 0)
    peers = peers + jnp.where(is_worker, NSUP, 0) - jnp.where(own_worker, 2, 0)
    pl.semaphore_wait(barrier, peers)

    def chunk(path, zz, pos, h=None):
        inner = pl.ds(0, 4) if h is None else pl.ds(2 * h, 2)
        if path == 0:
            return kbuf.at[zz, pos, inner, pl.ds(0, HALF)]
        return kbuf.at[zz, inner, pos, pl.ds(HALF, HALF)]

    pos = (y, x)

    def last_dev(path, k):
        if path == 0:
            return device(z, (y + k) % NY, x, 0)
        return device(z, y, (x + k) % NX, 0)

    @pl.when(core == 0)
    def _():
        for k in range(1, 4):
            own = kbuf.at[z, y, x, pl.ds(0, HALF)]
            send(own, own, fs.at[0, k - 1], fr.at[0, k - 1], device(z, y, (x + k) % NX, 0))
            own = kbuf.at[z, y, x, pl.ds(HALF, HALF)]
            send(own, own, fs.at[1, k - 1], fr.at[1, k - 1], device(z, (y + k) % NY, x, 0))

    def send_label(j, c):
        to = to_worker(j)

        @pl.when((core == 1) | (to != sup))
        def _():
            send(stage.at[j, pl.ds(0, SENT)], bbuf.at[sup, pl.ds(0, SENT)], ls, lr, {"sup": to, "cls": x * 2})

        return c

    lax.fori_loop(0, BLOCKS, send_label, 0)

    @pl.when(own_worker)
    def _():
        bbuf[sup] = stage[block]

    @pl.when(core == 0)
    def _():
        def forward(path, zz):
            me = pos[path]
            arrive(chunk(path, zz, me), dr.at[path, 0, zz])
            ref = chunk(path, zz, (me + 3) % 4, 0)
            send(ref, ref, ws.at[path, 0], wr.at[path, 0, zz], last_dev(path, 1))
            arrive(chunk(path, zz, me), dr.at[path, 1, zz])
            ref = chunk(path, zz, (me + 1) % 4, 1)
            send(ref, ref, ws.at[path, 1], wr.at[path, 1, zz], last_dev(path, 3))

        def having(k):
            if k == 0:
                return [z]
            if k == NZ // 2:
                return [(z + k) % NZ]
            return [(z + NZ - k) % NZ, (z + k) % NZ]

        last = NZ // 2
        for k in range(last + 2):
            for path in range(2):
                me = pos[path]
                if k <= last:
                    if k == 0:
                        for i in range(3):
                            arrive(kbuf.at[z, y, x, pl.ds(0, HALF)], fr.at[path, i])
                    else:
                        h = None if k < last else 0
                        arrive(chunk(path, z, me, h), zr.at[path, 0, k - 1])
                        arrive(chunk(path, z, me, h), zr.at[path, 1, k - 1])
                    if k < last:
                        right = chunk(path, (z + NZ - k) % NZ, me, None if k < last - 1 else 0)
                        left = chunk(path, (z + k) % NZ, me, None if k < last - 1 else 1)
                        send(right, right, zs.at[path, 0], zr.at[path, 0, k], device(up, y, x, 0))
                        send(left, left, zs.at[path, 1], zr.at[path, 1, k], device(down, y, x, 0))
                    for zz in having(k):
                        ref = chunk(path, zz, me)
                        send(ref, ref, ds.at[path, 0], dr.at[path, 0, zz], last_dev(path, 1))
                        send(ref, ref, ds.at[path, 1], dr.at[path, 1, zz], last_dev(path, 3))
                if k > 0:
                    for zz in having(k - 1):
                        forward(path, zz)
        for path in range(2):
            for zz in range(NZ):
                arrive(chunk(path, zz, pos[path], 0), wr.at[path, 0, zz])
                arrive(chunk(path, zz, pos[path], 0), wr.at[path, 1, zz])

    @pl.when(is_worker)
    def _():
        @pl.when(served == 0)
        def _():
            arrive(bbuf.at[pl.ds(0, NSUP - 1), pl.ds(0, SENT)], lr)

        @pl.when(served == 1)
        def _():
            arrive(bbuf.at[:, pl.ds(0, SENT)], lr)

        def rows_of(r):
            return pl.ds(pl.multiple_of(r * 256, 256), 256)

        def product(r):
            lhs = jnp.concatenate(
                [kbuf[zz, r // 2, pl.ds((r % 2) * 2, 2), 0:LANES, :].reshape(256, LANES) for zz in range(NZ)], axis=1
            )
            return jnp.dot(lhs, pn[...].reshape(NZ * LANES, LANES), preferred_element_type=F32)

        def fold(v):
            return jnp.sum(v.reshape(32, 8, LANES), axis=0)

        def total(v):
            return jnp.sum(v, axis=0, keepdims=True)

        def to_natural(r, v):
            pn[pl.ds((r % 2) * 8, 8), r // 2] = v.reshape(8, ROWS, LANES).astype(BF16)

        zero = jnp.zeros((8, LANES), F32)

        def solve(emit):
            def first(r, c):
                image = product(r)
                b = bvec[rows_of(r), :]
                vec[rows_of(r), :] = image
                return c[0] + fold(b * b), c[1] + fold(b * image)

            norm, curve = lax.fori_loop(0, 8, first, (zero, zero))
            norm, curve = total(norm), total(curve)
            step0 = norm / curve

            def resid(r, c):
                v = bvec[rows_of(r), :] - step0 * vec[rows_of(r), :]
                vec[rows_of(r), :] = v
                return c + fold(v * v)

            norm1 = total(lax.fori_loop(0, 8, resid, zero))
            beta = norm1 / norm

            def turn(r, c):
                v = vec[rows_of(r), :] + beta * bvec[rows_of(r), :]
                dvec[rows_of(r), :] = v
                to_natural(r, v)
                return c

            lax.fori_loop(0, 8, turn, 0)

            def second(r, c):
                return c + fold(dvec[rows_of(r), :] * product(r))

            step1 = norm1 / total(lax.fori_loop(0, 8, second, zero))

            def finish(r, c):
                emit(r, step0 * bvec[rows_of(r), :] + step1 * dvec[rows_of(r), :])
                return c

            lax.fori_loop(0, 8, finish, 0)

        def load(r, c):
            b = bbuf.reshape(NZ, NY, CELL, LANES)[pl.ds((r % 2) * 8, 8), r // 2, 0:ROWS, :]
            bvec[rows_of(r), :] = b.reshape(256, LANES)
            pn[pl.ds((r % 2) * 8, 8), r // 2] = b.astype(BF16)
            return c

        lax.fori_loop(0, 8, load, 0)

        def keep_low(r, v):
            low[rows_of(r), :] = v.astype(BF16)

        solve(keep_low)

        crosses = [kbuf[:, q // NX, q % NX, LANES:PIECE, :].reshape(512, LANES) for q in range(16)]
        predicted = jnp.dot(jnp.concatenate(crosses, axis=1), low[...], preferred_element_type=F32)
        pred[...] = predicted.reshape(NSUP, TROWS, LANES)

        at = pl.ds(pl.multiple_of(block * LANES, LANES), LANES)

        def send_pred(s, c):
            @pl.when((served == 1) | (s != sup))
            def _():
                send(pred.at[s], pbuf.at[:, at], ps, pr, {"sup": s, "cls": x * 2 + served})

            return c

        lax.fori_loop(0, NSUP, send_pred, 0)

        @pl.when(served == 0)
        def _():
            pbuf[:, at] = pred[sup]

        lane = lax.broadcasted_iota(jnp.int32, (NSUP, TROWS, LANES), 2)
        row = lax.broadcasted_iota(jnp.int32, (NSUP, TROWS, LANES), 1)
        target = jnp.sum(jnp.where(lane == row, bbuf[:, ROWS : ROWS + 1, :], 0.0), axis=2, keepdims=True)
        first_class = ((x * 2 + served) * BLOCKS + block) * LANES
        onehot = jnp.where(target == (first_class + lane).astype(F32), LABEL_SCALE, 0.0)
        misfit = (predicted - onehot.reshape(512, LANES)).astype(BF16)
        for q in range(16):
            cross = kbuf[:, q // NX, q % NX, LANES:PIECE, :].reshape(512, LANES)
            rhs = lax.dot_general(cross, misfit, (((0,), (0,)), ((), ())), preferred_element_type=F32)
            bvec[q * LANES : (q + 1) * LANES, :] = rhs
            for a in range(4):
                pn[(q % NX) * 4 + a, q // NX] = rhs[a * ROWS : (a + 1) * ROWS].astype(BF16)

        def keep_hyper(r, v):
            hst[pl.ds((r % 2) * 8, 8), r // 2] = v.reshape(8, ROWS, LANES).astype(BF16)

        solve(keep_hyper)

        def send_hyper(s, c):
            @pl.when((served == 1) | (s != sup))
            def _():
                send(hst.at[s // NY, s % NY], hbuf.at[:, at], hs, hr, {"sup": s, "cls": x * 2 + served})

            return c

        lax.fori_loop(0, NSUP, send_hyper, 0)

        @pl.when(served == 0)
        def _():
            hbuf[:, at] = hst[z, y]

    def collect(buf, sem):
        @pl.when(own_worker)
        def _():
            arrive(buf.at[:, pl.ds(0, (BLOCKS - 1) * LANES)], sem)

        @pl.when(jnp.logical_not(own_worker))
        def _():
            arrive(buf, sem)

    collect(pbuf, pr)
    pred_out[...] = pbuf[...].astype(BF16)
    collect(hbuf, hr)
    hyper_out[...] = hbuf[...].astype(F32)

    @pl.when(own_worker)
    def _():
        arrive(stage.at[pl.ds(0, BLOCKS - 1), pl.ds(0, SENT)], ls)

    @pl.when(jnp.logical_not(own_worker))
    def _():
        arrive(stage.at[:, pl.ds(0, SENT)], ls)

    @pl.when(core == 0)
    def _():
        for path in range(2):
            for i in range(3):
                arrive(kbuf.at[z, y, x, pl.ds(0, HALF)], fs.at[path, i])
            for d in range(2):
                arrive(kbuf.at[pl.ds(0, NZ - 1), 0, pl.ds(0, 2), pl.ds(0, HALF)], zs.at[path, d])
                arrive(kbuf.at[:, 0, :, pl.ds(0, HALF)], ds.at[path, d])
                arrive(kbuf.at[:, 0, pl.ds(0, 2), pl.ds(0, HALF)], ws.at[path, d])

    @pl.when(is_worker & (served == 0))
    def _():
        arrive(pred.at[pl.ds(0, NSUP - 1)], ps)
        arrive(low.at[pl.ds(0, (NSUP - 1) * ROWS)], hs)

    @pl.when(is_worker & (served == 1))
    def _():
        arrive(pred, ps)
        arrive(hst, hs)


def vmem():
    return pl.BlockSpec(memory_space=pltpu.VMEM)


def local(support_feats, target_feats, scales, soft_labels, target_labels):
    width = support_feats.shape[1]
    dma = pltpu.SemaphoreType.DMA
    piece = pl.pallas_call(
        gram_kernel,
        out_shape=jax.ShapeDtypeStruct((PIECE, LANES), BF16),
        in_specs=[vmem()] * 3,
        out_specs=vmem(),
        scratch_shapes=[
            pltpu.VMEM((NZ, ROWS, width), BF16),
            pltpu.VMEM((NY, ROWS, width), BF16),
            pltpu.VMEM((NY, 16, width), BF16),
            pltpu.VMEM((NX, PIECE, LANES), F32),
            pltpu.VMEM((2 * NX, PIECE, LANES), F32),
            dma((2, NZ // 2)), dma((2, NZ // 2)),
            dma((NY - 1,)), dma((NY - 1,)), dma((NY - 1,)), dma((NY - 1,)),
            dma((NX,)), dma,
        ],
        compiler_params=pltpu.CompilerParams(collective_id=0, has_side_effects=True, vmem_limit_bytes=24 * 2**20),
        name="gram",
    )(support_feats, target_feats, scales.astype(F32).reshape(NZ, LANES))

    classes = jnp.zeros((CELL - ROWS, LANES), F32).at[:, 0:TROWS].set(target_labels.astype(F32)[None, :])
    return pl.pallas_call(
        solve_kernel,
        out_shape=(
            jax.ShapeDtypeStruct((TROWS, BLOCKS * LANES), BF16),
            jax.ShapeDtypeStruct((ROWS, BLOCKS * LANES), F32),
        ),
        in_specs=[vmem()] * 3,
        out_specs=(vmem(), vmem()),
        scratch_shapes=[
            pltpu.VMEM((NZ, NY, NX, PIECE, LANES), BF16),
            pltpu.VMEM((BLOCKS, CELL, LANES), F32),
            pltpu.VMEM((NSUP, CELL, LANES), F32),
            pltpu.VMEM((ROWS, BLOCKS * LANES), BF16),
            pltpu.VMEM((TROWS, BLOCKS * LANES), F32),
            pltpu.VMEM((NZ, NY, ROWS, LANES), BF16),
            pltpu.VMEM((2048, LANES), F32),
            pltpu.VMEM((2048, LANES), F32),
            pltpu.VMEM((2048, LANES), F32),
            pltpu.VMEM((2048, LANES), BF16),
            pltpu.VMEM((NSUP, TROWS, LANES), F32),
            pltpu.VMEM((NZ, NY, ROWS, LANES), BF16),
            dma, dma,
            dma((2, 3)), dma((2, 3)),
            dma((2, 2)), dma((2, 2, NZ // 2)),
            dma((2, 2)), dma((2, 2, NZ)),
            dma((2, 2)), dma((2, 2, NZ)),
            dma, dma, dma, dma,
        ],
        compiler_params=pltpu.CompilerParams(collective_id=1, has_side_effects=True, vmem_limit_bytes=44 * 2**20),
        name="solve",
    )(piece, soft_labels, classes)


def solution(mesh):
    in_specs = (P("sup", "cls"), P("sup", "cls"), P(), P("sup", "cls"), P("sup"))
    out_specs = (P("sup", "cls"), P("sup", "cls"))
    return jax.shard_map(local, mesh=mesh, in_specs=in_specs, out_specs=out_specs, check_vma=False)
```

```python
import functools

import jax
import jax.numpy as jnp
from jax import lax
from jax.experimental import pallas as pl
from jax.experimental.pallas import tpu as pltpu
from jax.sharding import PartitionSpec as P

MESH = pl.DeviceIdType.MESH
F = 8192
RIDGE = 0.05
LABEL_SCALE = 16.0

NZ, NY, NX = 16, 4, 4
NSUP = NZ * NY
ROWS = 32
TROWS = 8
LANES = 128
BLOCKS = 21
PIECE = LANES + NY * TROWS
HALF = PIECE // 2
KPART, CPART = LANES // 2, NY * TROWS // 2
WINDOW = (0, 1, -1, 2)
F32 = jnp.float32
BF16 = jnp.bfloat16


def place():
    sup = lax.axis_index("sup")
    cls = lax.axis_index("cls")
    return sup // NY, sup % NY, cls // 2, cls % 2


def device(z, y, x, core):
    return {"sup": z * NY + y, "cls": x * 2 + core}


def signal(sem, dev):
    pl.semaphore_signal(sem, inc=1, device_id=dev, device_id_type=MESH)


def send(src, dst, send_sem, recv_sem, dev):
    pltpu.make_async_remote_copy(
        src_ref=src, dst_ref=dst, send_sem=send_sem, recv_sem=recv_sem, device_id=dev, device_id_type=MESH
    ).start()


def arrive(ref, sem):
    pltpu.make_async_copy(ref, ref, sem).wait()


def worker_sup(w, x):
    v = (w * 8) // 7
    return (v // 3) * NY + (v % 3 + 8 - x) % NY


def kernel(
    feats, targets, scales, labels, classes, pbuf, hbuf,
    ibuf, tbuf, jbuf, part, rbuf, kbuf, cstage, cbuf, bbuf, pn, bvec, vec, low, pred, hst,
    wide, iws, iwr, tws, twr, iys, iyr, tys, tyr, js, jr, xs, xr,
    ls, lr, cs, cr, s1, r1, s2, r2, s4, r4, s5, r5, s6, r6, s7, ps, pr, hs, hr,
):
    z, y, x, core = place()
    sup = z * NY + y
    zq, zr = z // 4, z % 4
    kind = (y + x) % 4
    v = z * 3 + kind
    w = (v * 7 + 7) // 8
    is_worker = (core == 0) & (kind < 3) & ((w * 8) // 7 == v) & (w < 2 * BLOCKS)
    served = w // BLOCKS
    block = w % BLOCKS
    own_worker = is_worker & (served == 0)
    others = jnp.logical_not(own_worker)

    def zshift(d):
        return (z + NZ + d) % NZ

    barrier = pltpu.get_barrier_semaphore()
    for t in range(1, 4):
        signal(barrier, device(zshift(WINDOW[t]), y, x, core))
        signal(barrier, device(zshift(4 * t), y, x, core))
        signal(barrier, device(z, (y + t) % NY, x, core))

    @pl.when(core == 0)
    def _():
        for t in range(1, 4):
            signal(barrier, device(z, y, (x + t) % NX, 0))
            signal(barrier, device(z, y, (x + t) % NX, 1))
            signal(barrier, device(zshift(4 * t), y, x, 1))
        signal(barrier, device(z, y, x, 1))

    own_window = pltpu.make_async_copy(feats, ibuf.at[0, y], s7)
    own_stride = pltpu.make_async_copy(feats, jbuf.at[zq], s1)
    own_window.start()
    own_stride.start()
    tf = targets[...].astype(F32)
    half = tf.shape[1] // 2
    tbuf[0, y] = jnp.concatenate([tf[:, :half], tf[:, half:]], axis=0).astype(BF16)
    lane8 = lax.broadcasted_iota(jnp.int32, (8, LANES), 1)
    row8 = jnp.zeros((8, LANES), jnp.int32)
    for i in range(TROWS):
        row8 = jnp.where(lane8 == i, classes[i], row8)
    cstage[...] = row8.astype(F32)
    wide[...] = scales[...].astype(F32)

    own_window.wait()
    own_stride.wait()
    pl.semaphore_wait(barrier, 3 * 4 + 4 * core)

    def spread(t, i):
        dev = device(z, (y + i) % NY, x, core)
        send(ibuf.at[t, y], ibuf.at[t, y], iys.at[t, i - 1], iyr.at[t, i - 1], dev)
        send(tbuf.at[t, y], tbuf.at[t, y], tys.at[t, i - 1], tyr.at[t, i - 1], dev)

    for t in range(1, 4):
        dev = device(zshift(-WINDOW[t]), y, x, core)
        send(ibuf.at[0, y], ibuf.at[t, y], iws.at[t - 1], iwr.at[t - 1], dev)
        send(tbuf.at[0, y], tbuf.at[t, y], tws.at[t - 1], twr.at[t - 1], dev)
        spread(0, t)
    for i in (2, 1, 3):
        send(jbuf.at[zq], jbuf.at[zq], js.at[i - 1], jr.at[i - 1], device(zshift(4 * i), y, x, core))
    for t in range(1, 4):
        arrive(ibuf.at[t, y], iwr.at[t - 1])
        arrive(tbuf.at[t, y], twr.at[t - 1])
        for i in range(1, 4):
            spread(t, i)
    for i in range(3):
        arrive(jbuf.at[zq], jr.at[i])
    for t in range(4):
        for i in range(3):
            arrive(ibuf.at[t, y], iyr.at[t, i])
            arrive(tbuf.at[t, y], tyr.at[t, i])

    over = (((1,), (1,)), ((), ()))
    own = x * 2 + core
    cols = jbuf[...].reshape(4 * ROWS, -1)
    for t in range(NX):
        part[t, 0:LANES] = lax.dot_general(
            cols, ibuf[t].reshape(NY * ROWS, -1), over, preferred_element_type=F32
        )
        low_t = tbuf[t].reshape(NY * 16, half)
        cross0 = lax.dot_general(low_t, cols[:, :half], over, preferred_element_type=F32)
        cross1 = lax.dot_general(low_t, cols[:, half:], over, preferred_element_type=F32)
        cross = cross0.reshape(NY, 16, LANES)[:, :TROWS] + cross1.reshape(NY, 16, LANES)[:, TROWS:]
        part[t, LANES:PIECE] = cross.reshape(NY * TROWS, LANES)

        @pl.when((core == 1) | (x != t))
        def _():
            send(part.at[t], rbuf.at[own], xs, xr, device(z, y, t, 0))

    def send_label(i, c):
        j = ((sup * 21) // 64 + i) % BLOCKS
        to = worker_sup(core * BLOCKS + j, x)

        @pl.when((core == 1) | (to != sup))
        def _():
            dev = {"sup": to, "cls": x * 2}
            send(labels.at[:, pl.ds(pl.multiple_of(j * LANES, LANES), LANES)], bbuf.at[sup], ls, lr, dev)
            send(cstage.at[pl.ds(0, 1)], cbuf.at[sup, pl.ds(0, 1)], cs, cr, dev)

        return c

    def send_labels():
        lax.fori_loop(0, BLOCKS, send_label, 0)

    pl.when(core == 1)(send_labels)

    @pl.when(own_worker)
    def _():
        own_labels = pltpu.make_async_copy(
            labels.at[:, pl.ds(pl.multiple_of(block * LANES, LANES), LANES)], bbuf.at[sup], s7
        )
        own_labels.start()
        own_labels.wait()
        cbuf[sup] = cstage[...]

    @pl.when(core == 0)
    def _():
        gather_pieces(
            z, y, x, zq, zr, kind, zshift, send_labels, wide, part, rbuf, kbuf, xr, own,
            s1, r1, s2, r2, s4, r4, s5, r5, s6, r6,
        )

    def arrive_rows(t):
        for path in range(2):
            for i in range(3):
                arrive(kbuf.at[:, 0, y, :, pl.ds(0, KPART)], r4.at[path, i, t])

    lanes_at = pl.ds(pl.multiple_of(block * LANES, LANES), LANES)

    @pl.when(is_worker)
    def _():
        @pl.when(served == 0)
        def _():
            arrive(bbuf.at[pl.ds(0, NSUP - 1)], lr)
            arrive(cbuf.at[pl.ds(0, NSUP - 1), pl.ds(0, 1)], cr)

        @pl.when(served == 1)
        def _():
            arrive(bbuf, lr)
            arrive(cbuf.at[:, pl.ds(0, 1)], cr)

        def client(kk, q):
            return kk * 16 + q

        def rows_of(rho):
            return pl.ds(pl.multiple_of(rho * 512, 512), 512)

        def product(rho):
            order = [(a, b) for a in range(4) for b in range(NX)]
            rhs = jnp.concatenate(
                [pn[(a * 4 + rho + WINDOW[b] + NZ) % NZ].reshape(LANES, LANES) for a, b in order], axis=0
            )
            rows = []
            for yy in range(NY):
                for h in range(2):
                    part_rows = pl.ds(h * HALF, KPART)
                    rows.append(jnp.concatenate([kbuf[a, rho, yy, b, part_rows, :] for a, b in order], axis=1))
            return jnp.dot(jnp.concatenate(rows, axis=0), rhs, preferred_element_type=F32)

        def fold(v):
            return jnp.sum(v.reshape(64, 8, LANES), axis=0)

        def total(v):
            return jnp.sum(v, axis=0, keepdims=True)

        def to_blocks(ref, rho, v):
            v = v.reshape(NY, 4, ROWS, LANES).astype(BF16)
            for yy in range(NY):
                for kk in range(4):
                    ref[kk * 4 + rho, yy] = v[yy, kk]

        zero = jnp.zeros((8, LANES), F32)

        def solve(emit, order=None):
            def first(t, c):
                rho = t
                if order is not None:
                    rho = (z + WINDOW[t] + 4) % 4
                    arrive_rows(t)
                image = product(rho)
                b = bvec[rows_of(rho), :]
                vec[rows_of(rho), :] = image
                return c[0] + fold(b * b), c[1] + fold(b * image)

            if order is None:
                norm, curve = lax.fori_loop(0, 4, first, (zero, zero))
            else:
                norm, curve = zero, zero
                for t in order:
                    norm, curve = first(t, (norm, curve))
            norm, curve = total(norm), total(curve)
            step0 = norm / curve

            def resid(rho, c):
                v = bvec[rows_of(rho), :] - step0 * vec[rows_of(rho), :]
                vec[rows_of(rho), :] = v
                return c + fold(v * v)

            norm1 = total(lax.fori_loop(0, 4, resid, zero))
            beta = norm1 / norm

            def turn(rho, c):
                v = vec[rows_of(rho), :] + beta * bvec[rows_of(rho), :]
                vec[rows_of(rho), :] = v
                to_blocks(pn, rho, v)
                return c

            lax.fori_loop(0, 4, turn, 0)

            def second(rho, c):
                return c + fold(vec[rows_of(rho), :] * product(rho))

            step1 = norm1 / total(lax.fori_loop(0, 4, second, zero))

            def finish(i, c):
                rho = (zr + i) % 4
                emit(rho, step0 * bvec[rows_of(rho), :] + step1 * vec[rows_of(rho), :])
                return c

            lax.fori_loop(0, 4, finish, 0)

        def load(s, c):
            b = bbuf[s]
            bvec[pl.ds(pl.multiple_of(((s % 16) * 4 + s // 16) * ROWS, ROWS), ROWS), :] = b
            pn[s // 4, s % 4] = b.astype(BF16)
            return c

        lax.fori_loop(0, NSUP, load, 0)

        def keep_low(rho, v):
            low[rows_of(rho), :] = v.astype(BF16)

        solve(keep_low, range(4))

        for path in range(2):
            for i in range(3):
                arrive(kbuf.at[:, :, 0, :, pl.ds(KPART, CPART)], r5.at[path, i])

        def cross_block(q):
            rho, yy = q // 4, q % 4
            blocks = []
            for zc in range(NZ):
                b = next(i for i in range(NX) if (zc - WINDOW[i] - rho) % 4 == 0)
                zz = (zc - WINDOW[b]) % NZ
                for h in range(2):
                    blocks.append(kbuf[zz // 4, rho, yy, b, h * HALF + KPART : (h + 1) * HALF, :])
            return jnp.concatenate(blocks, axis=0)

        predicted = jnp.dot(
            jnp.concatenate([cross_block(q) for q in range(16)], axis=1), low[...], preferred_element_type=F32
        )
        pred[...] = predicted.reshape(NSUP, TROWS, LANES)

        def send_pred(i, c):
            s = (sup + i) % NSUP

            @pl.when((served == 1) | (s != sup))
            def _():
                send(pred.at[s], pbuf.at[:, lanes_at], ps, pr, {"sup": s, "cls": x * 2 + served})

            return c

        lax.fori_loop(0, NSUP, send_pred, 0)

        @pl.when(served == 0)
        def _():
            pbuf[:, lanes_at] = pred[sup]

        lane = lax.broadcasted_iota(jnp.int32, (NSUP, TROWS, LANES), 2)
        row = lax.broadcasted_iota(jnp.int32, (NSUP, TROWS, LANES), 1)
        target = jnp.sum(jnp.where(lane == row, cbuf[:, 0:1, :], 0.0), axis=2, keepdims=True)
        first_class = ((x * 2 + served) * BLOCKS + block) * LANES
        onehot = jnp.where(target == (first_class + lane).astype(F32), LABEL_SCALE, 0.0)
        misfit = (predicted - onehot.reshape(NSUP * TROWS, LANES)).astype(BF16)
        for q in range(16):
            rhs = lax.dot_general(cross_block(q), misfit, (((0,), (0,)), ((), ())), preferred_element_type=F32)
            bvec[q * LANES : (q + 1) * LANES, :] = rhs
            for kk in range(4):
                pn[kk * 4 + q // 4, q % 4] = rhs[kk * ROWS : (kk + 1) * ROWS].astype(BF16)

        def keep_hyper(rho, v):
            to_blocks(hst, rho, v)

        solve(keep_hyper)

        def send_hyper(i, c):
            m = i // 4
            d = jnp.where(m % 2 == 0, 8 + m // 2, 7 - m // 2)
            zz, yy = (z + d) % NZ, (y + i + 2) % 4

            @pl.when((served == 1) | (zz != z) | (yy != y))
            def _():
                dev = {"sup": zz * NY + yy, "cls": x * 2 + served}
                send(hst.at[zz, yy], hbuf.at[:, lanes_at], hs, hr, dev)

            return c

        lax.fori_loop(0, NSUP, send_hyper, 0)

        @pl.when(served == 0)
        def _():
            hbuf[:, lanes_at] = hst[z, y]

    @pl.when((core == 0) & (kind < 3) & jnp.logical_not(is_worker))
    def _():
        for t in range(4):
            arrive_rows(t)
        for path in range(2):
            for i in range(3):
                arrive(kbuf.at[:, :, 0, :, pl.ds(KPART, CPART)], r5.at[path, i])

    def settle(buf, axis, sem, count):
        full, less = [slice(None)] * buf.ndim, [slice(None)] * buf.ndim
        less[axis] = pl.ds(0, (count - 1) * (buf.shape[axis] // count))

        @pl.when(own_worker)
        def _():
            arrive(buf.at[tuple(less)], sem)

        @pl.when(others)
        def _():
            arrive(buf.at[tuple(full)], sem)

    for t in range(3):
        arrive(ibuf.at[0, y], iws.at[t])
        arrive(tbuf.at[0, y], tws.at[t])
        arrive(jbuf.at[zq], js.at[t])
        for k in range(4):
            arrive(ibuf.at[0, y], iys.at[k, t])
            arrive(tbuf.at[0, y], tys.at[k, t])
    settle(labels, 1, ls, BLOCKS)

    @pl.when(own_worker)
    def _():
        arrive(cbuf.at[pl.ds(0, BLOCKS - 1), pl.ds(0, 1)], cs)

    @pl.when(others)
    def _():
        arrive(cbuf.at[pl.ds(0, BLOCKS), pl.ds(0, 1)], cs)

    @pl.when(core == 0)
    def _():
        arrive(part.at[pl.ds(0, NX - 1)], xs)
        arrive(kbuf.at[0, 0, 0, pl.ds(0, 3)], s1)
        arrive(kbuf.at[:, 0, 0, pl.ds(0, 3)], s6)
        for path in range(2):
            arrive(kbuf.at[:, 0, pl.ds(0, 3), :, pl.ds(0, HALF)], s2.at[path])

            def sent(count):
                arrive(kbuf.at[:, :, pl.ds(0, count), :, pl.ds(0, KPART)], s4.at[path])
                arrive(kbuf.at[:, :, pl.ds(0, count), :, pl.ds(KPART, CPART)], s5.at[path])

            pl.when(kind < 3)(functools.partial(sent, 2))
            pl.when(kind == 3)(functools.partial(sent, 3))

    @pl.when(core == 1)
    def _():
        arrive(part, xs)

    @pl.when(is_worker & (served == 0))
    def _():
        arrive(pred.at[pl.ds(0, NSUP - 1)], ps)
        arrive(low.at[pl.ds(0, (NSUP - 1) * ROWS)], hs)

    @pl.when(is_worker & (served == 1))
    def _():
        arrive(pred, ps)
        arrive(low, hs)

    settle(pbuf, 1, pr, BLOCKS)
    settle(hbuf, 1, hr, BLOCKS)


def gather_pieces(
    z, y, x, zq, zr, kind, zshift, send_labels, scales, part, rbuf, kbuf, xr, own,
    s1, r1, s2, r2, s4, r4, s5, r5, s6, r6,
):
    rbuf[own] = part[x]
    arrive(rbuf.at[pl.ds(0, 2 * NX - 1)], xr)
    summed = rbuf[0]
    for k in range(1, 2 * NX):
        summed = summed + rbuf[k]
    zc = zshift(jnp.where(x < 2, x, jnp.where(x == 2, WINDOW[2], WINDOW[3])))
    col_scale = scales[pl.ds(zc, 1), :]
    lane = lax.broadcasted_iota(jnp.int32, (ROWS, LANES), 1)
    row = lax.broadcasted_iota(jnp.int32, (ROWS, LANES), 0)
    row_scales = []
    for kk in range(4):
        zz = kk * 4 + zr
        picked = jnp.where(lane == y * ROWS + row, scales[pl.ds(zz, 1), :], 0.0)
        row_scale = jnp.sum(picked, axis=1, keepdims=True)
        row_scales.append(row_scale)
        diag = zz * LANES + y * ROWS + row == zc * LANES + lane
        block = summed[kk * ROWS : (kk + 1) * ROWS] * (row_scale * col_scale) / F
        at = (kk // 2) * HALF + (kk % 2) * ROWS
        kbuf[zq, zr, y, x, at : at + ROWS] = (block + jnp.where(diag, RIDGE, 0.0)).astype(BF16)
    row_scale = jnp.concatenate(row_scales, axis=0)
    same = lax.broadcasted_iota(jnp.int32, (LANES, LANES), 0) == lax.broadcasted_iota(jnp.int32, (LANES, LANES), 1)
    cross_scale = jnp.sum(jnp.where(same, row_scale, 0.0), axis=0, keepdims=True)
    for h in range(2):
        cross = summed[LANES + h * CPART : LANES + (h + 1) * CPART] * cross_scale / F
        kbuf[zq, zr, y, x, h * HALF + KPART : (h + 1) * HALF] = cross.astype(BF16)

    pos = (y, x)

    def last_dev(path, k):
        if path == 0:
            return device(z, (y + k) % NY, x, 0)
        return device(z, y, (x + k) % NX, 0)

    def line(path, k):
        if path == 0:
            return device(z, y, (x + k) % NX, 0)
        return device(z, (y + k) % NY, x, 0)

    def rho_of(t):
        return (z + WINDOW[t] + 4) % 4

    def window_send(ref, send_sem, recv_sems, ts):
        for t in ts:
            send(ref, ref, send_sem, recv_sems.at[t - 1], device(zshift(-WINDOW[t]), y, x, 0))

    piece = kbuf.at[zq, zr, y, x]
    for i in range(1, 4):
        send(piece, piece, s1, r1.at[i - 1], device(zshift(4 * i), y, x, 0))
    window_send(piece, s6, r6, (1, 2, 3))
    for i in range(1, 4):
        arrive(piece, r1.at[i - 1])
        window_send(kbuf.at[(zq + 4 - i) % 4, zr, y, x], s6, r6, (1, 2, 3))
    def middle(t):
        for i in (1, 3, 2):
            for path in range(2):
                ref = kbuf.at[:, rho_of(t), y, x, pl.ds(path * HALF, HALF)]
                send(ref, ref, s2.at[path], r2.at[path, i - 1, t], line(path, i))

    middle(0)
    send_labels()
    for t in range(1, 4):
        arrive(kbuf.at[:, 0, y, x], r6.at[t - 1])
        middle(t)

    def last(t):
        rho = rho_of(t)
        for a in range(2):
            refs = (
                kbuf.at[pl.ds(2 * a, 2), rho, y, :, pl.ds(0, KPART)],
                kbuf.at[pl.ds(2 * a, 2), rho, :, x, pl.ds(HALF, KPART)],
            )
            for i in (1, 3, 2):

                @pl.when((kind + i) % 4 < 3)
                def _():
                    for path in range(2):
                        send(refs[path], refs[path], s4.at[path], r4.at[path, i - 1, t], last_dev(path, i))

    for t in range(4):
        for path in range(2):
            for i in range(3):
                arrive(kbuf.at[:, 0, y, x, pl.ds(0, HALF)], r2.at[path, i, t])
        last(t)
    refs = (kbuf.at[:, :, y, :, pl.ds(KPART, CPART)], kbuf.at[:, :, :, x, pl.ds(HALF + KPART, CPART)])
    for i in (1, 3, 2):

        @pl.when((kind + i) % 4 < 3)
        def _():
            for path in range(2):
                send(refs[path], refs[path], s5.at[path], r5.at[path, i - 1], last_dev(path, i))


def local(support_feats, target_feats, scales, soft_labels, target_labels):
    width = support_feats.shape[1]
    dma = pltpu.SemaphoreType.DMA
    vmem = pl.BlockSpec(memory_space=pltpu.VMEM)
    pred, hyper = pl.pallas_call(
        kernel,
        out_shape=(
            jax.ShapeDtypeStruct((TROWS, BLOCKS * LANES), F32),
            jax.ShapeDtypeStruct((ROWS, BLOCKS * LANES), BF16),
        ),
        in_specs=[pl.BlockSpec(memory_space=pl.ANY), vmem, vmem, pl.BlockSpec(memory_space=pl.ANY), pl.BlockSpec(memory_space=pltpu.SMEM)],
        out_specs=(vmem, vmem),
        scratch_shapes=[
            pltpu.VMEM((4, NY, ROWS, width), BF16),
            pltpu.VMEM((4, NY, 16, width // 2), BF16),
            pltpu.VMEM((4, ROWS, width), BF16),
            pltpu.VMEM((NX, PIECE, LANES), F32),
            pltpu.VMEM((2 * NX, PIECE, LANES), F32),
            pltpu.VMEM((4, 4, NY, NX, PIECE, LANES), BF16),
            pltpu.VMEM((8, LANES), F32),
            pltpu.VMEM((NSUP, 8, LANES), F32),
            pltpu.VMEM((NSUP, ROWS, LANES), F32),
            pltpu.VMEM((NZ, NY, ROWS, LANES), BF16),
            pltpu.VMEM((2048, LANES), F32),
            pltpu.VMEM((2048, LANES), F32),
            pltpu.VMEM((2048, LANES), BF16),
            pltpu.VMEM((NSUP, TROWS, LANES), F32),
            pltpu.VMEM((NZ, NY, ROWS, LANES), BF16),
            pltpu.VMEM((NZ, LANES), F32),
            dma((3,)), dma((3,)), dma((3,)), dma((3,)),
            dma((4, 3)), dma((4, 3)), dma((4, 3)), dma((4, 3)),
            dma((3,)), dma((3,)), dma, dma,
            dma, dma, dma, dma,
            dma, dma((3,)), dma((2,)), dma((2, 3, 4)),
            dma((2,)), dma((2, 3, 4)), dma((2,)), dma((2, 3)), dma, dma((3,)), dma,
            dma, dma, dma, dma,
        ],
        compiler_params=pltpu.CompilerParams(collective_id=0, has_side_effects=True, vmem_limit_bytes=56 * 2**20),
        name="hypergradient",
    )(support_feats, target_feats, scales.reshape(NZ, LANES), soft_labels, target_labels)
    return pred.astype(BF16), hyper.astype(F32)


def solution(mesh):
    in_specs = (P("sup", "cls"), P("sup", "cls"), P(), P("sup", "cls"), P("sup"))
    out_specs = (P("sup", "cls"), P("sup", "cls"))
    return jax.shard_map(local, mesh=mesh, in_specs=in_specs, out_specs=out_specs, check_vma=False)
```

```python
import functools

import jax
import jax.numpy as jnp
from jax import lax
from jax.experimental import pallas as pl
from jax.experimental.pallas import tpu as pltpu
from jax.sharding import PartitionSpec as P

MESH = pl.DeviceIdType.MESH
F = 8192
RIDGE = 0.05
LABEL_SCALE = 16.0

NZ, NY, NX = 16, 4, 4
NSUP = NZ * NY
ROWS = 32
TROWS = 8
LANES = 128
BLOCKS = 21
PIECE = LANES + NY * TROWS
HALF = PIECE // 2
KPART, CPART = LANES // 2, NY * TROWS // 2
WINDOW = (0, 1, -1, 2)
UNROLL = 4
F32 = jnp.float32
BF16 = jnp.bfloat16


def place():
    sup = lax.axis_index("sup")
    cls = lax.axis_index("cls")
    return sup // NY, sup % NY, cls // 2, cls % 2


def device(z, y, x, core):
    return {"sup": z * NY + y, "cls": x * 2 + core}


def signal(sem, dev):
    pl.semaphore_signal(sem, inc=1, device_id=dev, device_id_type=MESH)


def send(src, dst, send_sem, recv_sem, dev):
    pltpu.make_async_remote_copy(
        src_ref=src, dst_ref=dst, send_sem=send_sem, recv_sem=recv_sem, device_id=dev, device_id_type=MESH
    ).start()


def arrive(ref, sem):
    pltpu.make_async_copy(ref, ref, sem).wait()


def worker_sup(w, x):
    v = (w * 8) // 7
    return (v // 3) * NY + (v % 3 + 8 - x) % NY


def kernel(
    feats, targets, scales, labels, classes, pbuf, hbuf,
    ibuf, tbuf, jbuf, part, rbuf, kbuf, cstage, cbuf, bbuf, pn, bvec, vec, low, pred, hst,
    wide, go, iws, iwr, tws, twr, iys, iyr, tys, tyr, js, jr, xs, xr,
    ls, lr, cs, cr, s1, r1, s2, r2, s4, r4, s5, r5, s6, r6, s7, ps, pr, hs, hr,
):
    z, y, x, core = place()
    sup = z * NY + y
    zq, zr = z // 4, z % 4
    kind = (y + x) % 4
    v = z * 3 + kind
    w = (v * 7 + 7) // 8
    is_worker = (core == 0) & (kind < 3) & ((w * 8) // 7 == v) & (w < 2 * BLOCKS)
    served = w // BLOCKS
    block = w % BLOCKS
    own_worker = is_worker & (served == 0)
    others = jnp.logical_not(own_worker)

    def zshift(d):
        return (z + NZ + d) % NZ

    barrier = pltpu.get_barrier_semaphore()
    for t in range(1, 4):
        signal(barrier, device(zshift(WINDOW[t]), y, x, core))
        signal(barrier, device(z, (y + t) % NY, x, core))
    signal(barrier, device(zshift(4), y, x, core))
    signal(barrier, device(zshift(-4), y, x, core))

    @pl.when(core == 0)
    def _():
        for t in range(1, 4):
            signal(barrier, device(z, y, (x + t) % NX, 0))
            signal(barrier, device(z, y, (x + t) % NX, 1))
        signal(barrier, device(z, y, x, 1))

    own_window = pltpu.make_async_copy(feats, ibuf.at[0, y], s7)
    own_stride = pltpu.make_async_copy(feats, jbuf.at[zq], s1)
    own_window.start()
    own_stride.start()
    tf = targets[...].astype(F32)
    half = tf.shape[1] // 2
    tbuf[0, y] = jnp.concatenate([tf[:, :half], tf[:, half:]], axis=0).astype(BF16)
    lane8 = lax.broadcasted_iota(jnp.int32, (8, LANES), 1)
    row8 = jnp.zeros((8, LANES), jnp.int32)
    for i in range(TROWS):
        row8 = jnp.where(lane8 == i, classes[i], row8)
    cstage[...] = row8.astype(F32)
    wide[...] = scales[...].astype(F32)

    own_window.wait()
    own_stride.wait()
    pl.semaphore_wait(barrier, 3 * 3 + 2 + core)

    def spread(t, i):
        dev = device(z, (y + i) % NY, x, core)
        send(ibuf.at[t, y], ibuf.at[t, y], iys.at[t, i - 1], iyr.at[t, i - 1], dev)
        send(tbuf.at[t, y], tbuf.at[t, y], tys.at[t, i - 1], tyr.at[t, i - 1], dev)

    for t in range(1, 4):
        dev = device(zshift(-WINDOW[t]), y, x, core)
        send(ibuf.at[0, y], ibuf.at[t, y], iws.at[t - 1], iwr.at[t - 1], dev)
        send(tbuf.at[0, y], tbuf.at[t, y], tws.at[t - 1], twr.at[t - 1], dev)
        spread(0, t)

    def stride_send(i):
        send(jbuf.at[zq], jbuf.at[zq], js.at[i - 1], jr.at[i - 1], device(zshift(4 * i), y, x, core))

    stride_send(1)
    stride_send(3)

    def window_in(t):
        arrive(ibuf.at[t, y], iwr.at[t - 1])
        arrive(tbuf.at[t, y], twr.at[t - 1])
        for i in range(1, 4):
            spread(t, i)

    def stride_on(i, slot, start, to):
        arrive(jbuf.at[zq], jr.at[i])
        ref = jbuf.at[slot % 4, pl.ds(start, ROWS // 2)]
        send(ref, ref, js.at[i + 1], jr.at[i + 1], device(zshift(to), y, x, core))

    window_in(1)
    window_in(2)
    stride_on(0, zq + 3, 0, 4)
    stride_on(2, zq + 1, ROWS // 2, -4)
    window_in(3)
    arrive(jbuf.at[zq, pl.ds(0, ROWS // 2)], jr.at[1])
    arrive(jbuf.at[zq, pl.ds(0, ROWS // 2)], jr.at[3])
    for t in range(4):
        for i in range(3):
            arrive(ibuf.at[t, y], iyr.at[t, i])
            arrive(tbuf.at[t, y], tyr.at[t, i])

    over = (((1,), (1,)), ((), ()))
    own = x * 2 + core
    cols = jbuf[...].reshape(4 * ROWS, -1)
    for t in range(NX):
        part[t, 0:LANES] = lax.dot_general(
            cols, ibuf[t].reshape(NY * ROWS, -1), over, preferred_element_type=F32
        )
        low_t = tbuf[t].reshape(NY * 16, half)
        cross0 = lax.dot_general(low_t, cols[:, :half], over, preferred_element_type=F32)
        cross1 = lax.dot_general(low_t, cols[:, half:], over, preferred_element_type=F32)
        cross = cross0.reshape(NY, 16, LANES)[:, :TROWS] + cross1.reshape(NY, 16, LANES)[:, TROWS:]
        part[t, LANES:PIECE] = cross.reshape(NY * TROWS, LANES)

        @pl.when((core == 1) | (x != t))
        def _():
            send(part.at[t], rbuf.at[own], xs, xr, device(z, y, t, 0))

    def send_label(i, c):
        j = ((sup * 21) // 64 + i) % BLOCKS
        to = worker_sup(core * BLOCKS + j, x)

        @pl.when((core == 1) | (to != sup))
        def _():
            dev = {"sup": to, "cls": x * 2}
            send(labels.at[:, pl.ds(pl.multiple_of(j * LANES, LANES), LANES)], bbuf.at[sup], ls, lr, dev)
            send(cstage.at[pl.ds(0, 1)], cbuf.at[sup, pl.ds(0, 1)], cs, cr, dev)

        return c

    def send_labels():
        lax.fori_loop(0, BLOCKS, send_label, 0, unroll=3)

    @pl.when(core == 1)
    def _():
        pl.semaphore_wait(go, 1)
        send_labels()

    @pl.when(own_worker)
    def _():
        own_labels = pltpu.make_async_copy(
            labels.at[:, pl.ds(pl.multiple_of(block * LANES, LANES), LANES)], bbuf.at[sup], s7
        )
        own_labels.start()
        own_labels.wait()
        cbuf[sup] = cstage[...]

    @pl.when(core == 0)
    def _():
        gather_pieces(
            z, y, x, zq, zr, kind, zshift, send_labels, go, wide, part, rbuf, kbuf, xr, own,
            s1, r1, s2, r2, s4, r4, s5, r5, s6, r6,
        )

    def arrive_rows(t):
        for path in range(2):
            for i in range(3):
                arrive(kbuf.at[:, 0, y, :, pl.ds(0, KPART)], r4.at[path, i, t])

    lanes_at = pl.ds(pl.multiple_of(block * LANES, LANES), LANES)

    @pl.when(is_worker)
    def _():
        @pl.when(served == 0)
        def _():
            arrive(bbuf.at[pl.ds(0, NSUP - 1)], lr)
            arrive(cbuf.at[pl.ds(0, NSUP - 1), pl.ds(0, 1)], cr)

        @pl.when(served == 1)
        def _():
            arrive(bbuf, lr)
            arrive(cbuf.at[:, pl.ds(0, 1)], cr)

        def client(kk, q):
            return kk * 16 + q

        def rows_of(rho):
            return pl.ds(pl.multiple_of(rho * 512, 512), 512)

        def product(rho):
            order = [(a, b) for a in range(4) for b in range(NX)]
            rhs = jnp.concatenate(
                [pn[(a * 4 + rho + WINDOW[b] + NZ) % NZ].reshape(LANES, LANES) for a, b in order], axis=0
            )
            rows = []
            for yy in range(NY):
                for h in range(2):
                    part_rows = pl.ds(h * HALF, KPART)
                    rows.append(jnp.concatenate([kbuf[a, rho, yy, b, part_rows, :] for a, b in order], axis=1))
            return jnp.dot(jnp.concatenate(rows, axis=0), rhs, preferred_element_type=F32)

        def fold(v):
            return jnp.sum(v.reshape(64, 8, LANES), axis=0)

        def total(v):
            return jnp.sum(v, axis=0, keepdims=True)

        def to_blocks(ref, rho, v):
            v = v.reshape(NY, 4, ROWS, LANES).astype(BF16)
            for yy in range(NY):
                for kk in range(4):
                    ref[kk * 4 + rho, yy] = v[yy, kk]

        zero = jnp.zeros((8, LANES), F32)

        def solve(emit, order=None):
            def first(t, c):
                rho = t
                if order is not None:
                    rho = (z + WINDOW[t] + 4) % 4
                    arrive_rows(t)
                image = product(rho)
                b = bvec[rows_of(rho), :]
                vec[rows_of(rho), :] = image
                return c[0] + fold(b * b), c[1] + fold(b * image)

            if order is None:
                norm, curve = lax.fori_loop(0, 4, first, (zero, zero))
            else:
                norm, curve = zero, zero
                for t in order:
                    norm, curve = first(t, (norm, curve))
            norm, curve = total(norm), total(curve)
            step0 = norm / curve

            def resid(rho, c):
                v = bvec[rows_of(rho), :] - step0 * vec[rows_of(rho), :]
                vec[rows_of(rho), :] = v
                return c + fold(v * v)

            norm1 = total(lax.fori_loop(0, 4, resid, zero))
            beta = norm1 / norm

            def turn(rho, c):
                v = vec[rows_of(rho), :] + beta * bvec[rows_of(rho), :]
                vec[rows_of(rho), :] = v
                to_blocks(pn, rho, v)
                return c

            lax.fori_loop(0, 4, turn, 0)

            def second(rho, c):
                return c + fold(vec[rows_of(rho), :] * product(rho))

            step1 = norm1 / total(lax.fori_loop(0, 4, second, zero))

            def finish(i, c):
                rho = (zr + i) % 4
                emit(rho, step0 * bvec[rows_of(rho), :] + step1 * vec[rows_of(rho), :])
                return c

            lax.fori_loop(0, 4, finish, 0)

        def load(s, c):
            b = bbuf[s]
            bvec[pl.ds(pl.multiple_of(((s % 16) * 4 + s // 16) * ROWS, ROWS), ROWS), :] = b
            pn[s // 4, s % 4] = b.astype(BF16)
            return c

        lax.fori_loop(0, NSUP, load, 0)

        def keep_low(rho, v):
            low[rows_of(rho), :] = v.astype(BF16)

        solve(keep_low, range(4))

        for path in range(2):
            for i in range(3):
                arrive(kbuf.at[:, :, 0, :, pl.ds(KPART, CPART)], r5.at[path, i])

        def cross_block(q):
            rho, yy = q // 4, q % 4
            blocks = []
            for zc in range(NZ):
                b = next(i for i in range(NX) if (zc - WINDOW[i] - rho) % 4 == 0)
                zz = (zc - WINDOW[b]) % NZ
                for h in range(2):
                    blocks.append(kbuf[zz // 4, rho, yy, b, h * HALF + KPART : (h + 1) * HALF, :])
            return jnp.concatenate(blocks, axis=0)

        predicted = jnp.dot(
            jnp.concatenate([cross_block(q) for q in range(16)], axis=1), low[...], preferred_element_type=F32
        )
        pred[...] = predicted.reshape(NSUP, TROWS, LANES)

        def send_pred(i, c):
            s = (sup + i) % NSUP

            @pl.when((served == 1) | (s != sup))
            def _():
                send(pred.at[s], pbuf.at[:, lanes_at], ps, pr, {"sup": s, "cls": x * 2 + served})

            return c

        lax.fori_loop(0, NSUP, send_pred, 0, unroll=UNROLL)

        @pl.when(served == 0)
        def _():
            pbuf[:, lanes_at] = pred[sup]

        lane = lax.broadcasted_iota(jnp.int32, (NSUP, TROWS, LANES), 2)
        row = lax.broadcasted_iota(jnp.int32, (NSUP, TROWS, LANES), 1)
        target = jnp.sum(jnp.where(lane == row, cbuf[:, 0:1, :], 0.0), axis=2, keepdims=True)
        first_class = ((x * 2 + served) * BLOCKS + block) * LANES
        onehot = jnp.where(target == (first_class + lane).astype(F32), LABEL_SCALE, 0.0)
        misfit = (predicted - onehot.reshape(NSUP * TROWS, LANES)).astype(BF16)
        for q in range(16):
            rhs = lax.dot_general(cross_block(q), misfit, (((0,), (0,)), ((), ())), preferred_element_type=F32)
            bvec[q * LANES : (q + 1) * LANES, :] = rhs
            for kk in range(4):
                pn[kk * 4 + q // 4, q % 4] = rhs[kk * ROWS : (kk + 1) * ROWS].astype(BF16)

        def keep_hyper(rho, v):
            to_blocks(hst, rho, v)

        solve(keep_hyper)

        def send_hyper(i, c):
            m = i // 4
            d = jnp.where(m % 2 == 0, 8 + m // 2, 7 - m // 2)
            zz, yy = (z + d) % NZ, (y + i + 2) % 4

            @pl.when((served == 1) | (zz != z) | (yy != y))
            def _():
                dev = {"sup": zz * NY + yy, "cls": x * 2 + served}
                send(hst.at[zz, yy], hbuf.at[:, lanes_at], hs, hr, dev)

            return c

        lax.fori_loop(0, NSUP, send_hyper, 0, unroll=UNROLL)

        @pl.when(served == 0)
        def _():
            hbuf[:, lanes_at] = hst[z, y]

    @pl.when((core == 0) & (kind < 3) & jnp.logical_not(is_worker))
    def _():
        for t in range(4):
            arrive_rows(t)
        for path in range(2):
            for i in range(3):
                arrive(kbuf.at[:, :, 0, :, pl.ds(KPART, CPART)], r5.at[path, i])

    def settle(buf, axis, sem, count):
        full, less = [slice(None)] * buf.ndim, [slice(None)] * buf.ndim
        less[axis] = pl.ds(0, (count - 1) * (buf.shape[axis] // count))

        @pl.when(own_worker)
        def _():
            arrive(buf.at[tuple(less)], sem)

        @pl.when(others)
        def _():
            arrive(buf.at[tuple(full)], sem)

    for t in range(3):
        arrive(ibuf.at[0, y], iws.at[t])
        arrive(tbuf.at[0, y], tws.at[t])
        for k in range(4):
            arrive(ibuf.at[0, y], iys.at[k, t])
            arrive(tbuf.at[0, y], tys.at[k, t])
    for i in range(2):
        arrive(jbuf.at[zq], js.at[2 * i])
        arrive(jbuf.at[zq, pl.ds(0, ROWS // 2)], js.at[2 * i + 1])
    settle(labels, 1, ls, BLOCKS)

    @pl.when(own_worker)
    def _():
        arrive(cbuf.at[pl.ds(0, BLOCKS - 1), pl.ds(0, 1)], cs)

    @pl.when(others)
    def _():
        arrive(cbuf.at[pl.ds(0, BLOCKS), pl.ds(0, 1)], cs)

    @pl.when(core == 0)
    def _():
        arrive(part.at[pl.ds(0, NX - 1)], xs)
        arrive(kbuf.at[0, 0, 0, pl.ds(0, 3)], s1)
        arrive(kbuf.at[:, 0, 0, pl.ds(0, 3)], s6)
        for path in range(2):
            arrive(kbuf.at[:, 0, pl.ds(0, 3), :, pl.ds(0, HALF)], s2.at[path])

            def sent(count):
                arrive(kbuf.at[:, :, pl.ds(0, count), :, pl.ds(0, KPART)], s4.at[path])
                arrive(kbuf.at[:, :, pl.ds(0, count), :, pl.ds(KPART, CPART)], s5.at[path])

            pl.when(kind < 3)(functools.partial(sent, 2))
            pl.when(kind == 3)(functools.partial(sent, 3))

    @pl.when(core == 1)
    def _():
        arrive(part, xs)

    @pl.when(is_worker & (served == 0))
    def _():
        arrive(pred.at[pl.ds(0, NSUP - 1)], ps)
        arrive(low.at[pl.ds(0, (NSUP - 1) * ROWS)], hs)

    @pl.when(is_worker & (served == 1))
    def _():
        arrive(pred, ps)
        arrive(low, hs)

    settle(pbuf, 1, pr, BLOCKS)
    settle(hbuf, 1, hr, BLOCKS)


def gather_pieces(
    z, y, x, zq, zr, kind, zshift, send_labels, go, scales, part, rbuf, kbuf, xr, own,
    s1, r1, s2, r2, s4, r4, s5, r5, s6, r6,
):
    rbuf[own] = part[x]
    arrive(rbuf.at[pl.ds(0, 2 * NX - 1)], xr)
    summed = rbuf[0]
    for k in range(1, 2 * NX):
        summed = summed + rbuf[k]
    zc = zshift(jnp.where(x < 2, x, jnp.where(x == 2, WINDOW[2], WINDOW[3])))
    col_scale = scales[pl.ds(zc, 1), :]
    lane = lax.broadcasted_iota(jnp.int32, (ROWS, LANES), 1)
    row = lax.broadcasted_iota(jnp.int32, (ROWS, LANES), 0)
    row_scales = []
    for kk in range(4):
        zz = kk * 4 + zr
        picked = jnp.where(lane == y * ROWS + row, scales[pl.ds(zz, 1), :], 0.0)
        row_scale = jnp.sum(picked, axis=1, keepdims=True)
        row_scales.append(row_scale)
        diag = zz * LANES + y * ROWS + row == zc * LANES + lane
        block = summed[kk * ROWS : (kk + 1) * ROWS] * (row_scale * col_scale) / F
        at = (kk // 2) * HALF + (kk % 2) * ROWS
        kbuf[zq, zr, y, x, at : at + ROWS] = (block + jnp.where(diag, RIDGE, 0.0)).astype(BF16)
    row_scale = jnp.concatenate(row_scales, axis=0)
    same = lax.broadcasted_iota(jnp.int32, (LANES, LANES), 0) == lax.broadcasted_iota(jnp.int32, (LANES, LANES), 1)
    cross_scale = jnp.sum(jnp.where(same, row_scale, 0.0), axis=0, keepdims=True)
    for h in range(2):
        cross = summed[LANES + h * CPART : LANES + (h + 1) * CPART] * cross_scale / F
        kbuf[zq, zr, y, x, h * HALF + KPART : (h + 1) * HALF] = cross.astype(BF16)

    pos = (y, x)

    def last_dev(path, k):
        if path == 0:
            return device(z, (y + k) % NY, x, 0)
        return device(z, y, (x + k) % NX, 0)

    def line(path, k):
        if path == 0:
            return device(z, y, (x + k) % NX, 0)
        return device(z, (y + k) % NY, x, 0)

    def rho_of(t):
        return (z + WINDOW[t] + 4) % 4

    def window_send(ref, send_sem, recv_sems, ts):
        for t in ts:
            send(ref, ref, send_sem, recv_sems.at[t - 1], device(zshift(-WINDOW[t]), y, x, 0))

    piece = kbuf.at[zq, zr, y, x]
    for i in range(1, 4):
        send(piece, piece, s1, r1.at[i - 1], device(zshift(4 * i), y, x, 0))
    window_send(piece, s6, r6, (1, 2, 3))
    for i in range(1, 4):
        arrive(piece, r1.at[i - 1])
        window_send(kbuf.at[(zq + 4 - i) % 4, zr, y, x], s6, r6, (1, 2, 3))
    def middle(t):
        for i in (1, 3, 2):
            for path in range(2):
                ref = kbuf.at[:, rho_of(t), y, x, pl.ds(path * HALF, HALF)]
                send(ref, ref, s2.at[path], r2.at[path, i - 1, t], line(path, i))

    middle(0)
    for t in range(1, 4):
        arrive(kbuf.at[:, 0, y, x], r6.at[t - 1])
        middle(t)
    signal(go, device(z, y, x, 1))

    def last(t):
        rho = rho_of(t)
        for a in range(2):
            refs = (
                kbuf.at[pl.ds(2 * a, 2), rho, y, :, pl.ds(0, KPART)],
                kbuf.at[pl.ds(2 * a, 2), rho, :, x, pl.ds(HALF, KPART)],
            )
            for i in (1, 3, 2):

                @pl.when((kind + i) % 4 < 3)
                def _():
                    for path in range(2):
                        send(refs[path], refs[path], s4.at[path], r4.at[path, i - 1, t], last_dev(path, i))

    for t in range(4):
        for path in range(2):
            for i in range(3):
                arrive(kbuf.at[:, 0, y, x, pl.ds(0, HALF)], r2.at[path, i, t])
        last(t)
        if t == 0:
            send_labels()
    refs = (kbuf.at[:, :, y, :, pl.ds(KPART, CPART)], kbuf.at[:, :, :, x, pl.ds(HALF + KPART, CPART)])
    for i in (1, 3, 2):

        @pl.when((kind + i) % 4 < 3)
        def _():
            for path in range(2):
                send(refs[path], refs[path], s5.at[path], r5.at[path, i - 1], last_dev(path, i))


def local(support_feats, target_feats, scales, soft_labels, target_labels):
    width = support_feats.shape[1]
    dma = pltpu.SemaphoreType.DMA
    vmem = pl.BlockSpec(memory_space=pltpu.VMEM)
    pred, hyper = pl.pallas_call(
        kernel,
        out_shape=(
            jax.ShapeDtypeStruct((TROWS, BLOCKS * LANES), F32),
            jax.ShapeDtypeStruct((ROWS, BLOCKS * LANES), BF16),
        ),
        in_specs=[pl.BlockSpec(memory_space=pl.ANY), vmem, vmem, pl.BlockSpec(memory_space=pl.ANY), pl.BlockSpec(memory_space=pltpu.SMEM)],
        out_specs=(vmem, vmem),
        scratch_shapes=[
            pltpu.VMEM((4, NY, ROWS, width), BF16),
            pltpu.VMEM((4, NY, 16, width // 2), BF16),
            pltpu.VMEM((4, ROWS, width), BF16),
            pltpu.VMEM((NX, PIECE, LANES), F32),
            pltpu.VMEM((2 * NX, PIECE, LANES), F32),
            pltpu.VMEM((4, 4, NY, NX, PIECE, LANES), BF16),
            pltpu.VMEM((8, LANES), F32),
            pltpu.VMEM((NSUP, 8, LANES), F32),
            pltpu.VMEM((NSUP, ROWS, LANES), F32),
            pltpu.VMEM((NZ, NY, ROWS, LANES), BF16),
            pltpu.VMEM((2048, LANES), F32),
            pltpu.VMEM((2048, LANES), F32),
            pltpu.VMEM((2048, LANES), BF16),
            pltpu.VMEM((NSUP, TROWS, LANES), F32),
            pltpu.VMEM((NZ, NY, ROWS, LANES), BF16),
            pltpu.VMEM((NZ, LANES), F32),
            pltpu.SemaphoreType.REGULAR,
            dma((3,)), dma((3,)), dma((3,)), dma((3,)),
            dma((4, 3)), dma((4, 3)), dma((4, 3)), dma((4, 3)),
            dma((4,)), dma((4,)), dma, dma,
            dma, dma, dma, dma,
            dma, dma((3,)), dma((2,)), dma((2, 3, 4)),
            dma((2,)), dma((2, 3, 4)), dma((2,)), dma((2, 3)), dma, dma((3,)), dma,
            dma, dma, dma, dma,
        ],
        compiler_params=pltpu.CompilerParams(collective_id=0, has_side_effects=True, vmem_limit_bytes=56 * 2**20),
        name="hypergradient",
    )(support_feats, target_feats, scales.reshape(NZ, LANES), soft_labels, target_labels)
    return pred.astype(BF16), hyper.astype(F32)


def solution(mesh):
    in_specs = (P("sup", "cls"), P("sup", "cls"), P(), P("sup", "cls"), P("sup"))
    out_specs = (P("sup", "cls"), P("sup", "cls"))
    return jax.shard_map(local, mesh=mesh, in_specs=in_specs, out_specs=out_specs, check_vma=False)
```

```python
import functools

import jax
import jax.numpy as jnp
from jax import lax
from jax.experimental import pallas as pl
from jax.experimental.pallas import tpu as pltpu
from jax.sharding import PartitionSpec as P

MESH = pl.DeviceIdType.MESH
F = 8192
RIDGE = 0.05
LABEL_SCALE = 16.0

NZ, NY, NX = 16, 4, 4
NSUP = NZ * NY
ROWS = 32
TROWS = 8
LANES = 128
BLOCKS = 21
PIECE = LANES + NY * TROWS
HALF = PIECE // 2
KPART, CPART = LANES // 2, NY * TROWS // 2
WINDOW = (0, 1, -1, 2)
UNROLL = 4
SPLIT = 2
LABELS_AFTER = 3
F32 = jnp.float32
BF16 = jnp.bfloat16


def place():
    sup = lax.axis_index("sup")
    cls = lax.axis_index("cls")
    return sup // NY, sup % NY, cls // 2, cls % 2


def device(z, y, x, core):
    return {"sup": z * NY + y, "cls": x * 2 + core}


def signal(sem, dev):
    pl.semaphore_signal(sem, inc=1, device_id=dev, device_id_type=MESH)


def send(src, dst, send_sem, recv_sem, dev):
    pltpu.make_async_remote_copy(
        src_ref=src, dst_ref=dst, send_sem=send_sem, recv_sem=recv_sem, device_id=dev, device_id_type=MESH
    ).start()


def arrive(ref, sem):
    pltpu.make_async_copy(ref, ref, sem).wait()


def worker_sup(w, x):
    v = (w * 8) // 7
    return (v // 3) * NY + (v % 3 + 8 - x) % NY


def kernel(
    feats, targets, scales, labels, classes, pbuf, hbuf,
    ibuf, tbuf, jbuf, part, rbuf, kbuf, cstage, cbuf, bbuf, pn, bvec, vec, low, pred, hst,
    wide, go, iws, iwr, tws, twr, iys, iyr, tys, tyr, js, jr, xs, xr,
    ls, lr, cs, cr, s1, r1, s2, r2, s4, r4, s5, r5, s6, r6, s7, ps, pr, hs, hr,
):
    z, y, x, core = place()
    sup = z * NY + y
    zq, zr = z // 4, z % 4
    kind = (y + x) % 4
    v = z * 3 + kind
    w = (v * 7 + 7) // 8
    is_worker = (core == 0) & (kind < 3) & ((w * 8) // 7 == v) & (w < 2 * BLOCKS)
    served = w // BLOCKS
    block = w % BLOCKS
    own_worker = is_worker & (served == 0)
    others = jnp.logical_not(own_worker)

    def zshift(d):
        return (z + NZ + d) % NZ

    barrier = pltpu.get_barrier_semaphore()
    for t in range(1, 4):
        signal(barrier, device(zshift(WINDOW[t]), y, x, core))
        signal(barrier, device(z, (y + t) % NY, x, core))
    signal(barrier, device(zshift(4), y, x, core))
    signal(barrier, device(zshift(-4), y, x, core))

    @pl.when(core == 0)
    def _():
        for t in range(1, 4):
            signal(barrier, device(z, y, (x + t) % NX, 0))
            signal(barrier, device(z, y, (x + t) % NX, 1))
        signal(barrier, device(z, y, x, 1))

    own_window = pltpu.make_async_copy(feats, ibuf.at[0, y], s7)
    own_stride = pltpu.make_async_copy(feats, jbuf.at[zq], s1)
    own_window.start()
    own_stride.start()
    tf = targets[...].astype(F32)
    half = tf.shape[1] // 2
    tbuf[0, y] = jnp.concatenate([tf[:, :half], tf[:, half:]], axis=0).astype(BF16)
    lane8 = lax.broadcasted_iota(jnp.int32, (8, LANES), 1)
    row8 = jnp.zeros((8, LANES), jnp.int32)
    for i in range(TROWS):
        row8 = jnp.where(lane8 == i, classes[i], row8)
    cstage[...] = row8.astype(F32)
    wide[...] = scales[...].astype(F32)

    own_window.wait()
    own_stride.wait()
    pl.semaphore_wait(barrier, 3 * 3 + 2 + core)

    def spread(t, i):
        dev = device(z, (y + i) % NY, x, core)
        send(ibuf.at[t, y], ibuf.at[t, y], iys.at[t, i - 1], iyr.at[t, i - 1], dev)
        send(tbuf.at[t, y], tbuf.at[t, y], tys.at[t, i - 1], tyr.at[t, i - 1], dev)

    for t in range(1, 4):
        dev = device(zshift(-WINDOW[t]), y, x, core)
        send(ibuf.at[0, y], ibuf.at[t, y], iws.at[t - 1], iwr.at[t - 1], dev)
        send(tbuf.at[0, y], tbuf.at[t, y], tws.at[t - 1], twr.at[t - 1], dev)
        spread(0, t)

    def stride_send(i):
        send(jbuf.at[zq], jbuf.at[zq], js.at[i - 1], jr.at[i - 1], device(zshift(4 * i), y, x, core))

    stride_send(1)
    stride_send(3)

    def window_in(t):
        arrive(ibuf.at[t, y], iwr.at[t - 1])
        arrive(tbuf.at[t, y], twr.at[t - 1])
        for i in range(1, 4):
            spread(t, i)

    def stride_on(i, slot, start, to):
        arrive(jbuf.at[zq], jr.at[i])
        ref = jbuf.at[slot % 4, pl.ds(start, ROWS // 2)]
        send(ref, ref, js.at[i + 1], jr.at[i + 1], device(zshift(to), y, x, core))

    window_in(1)
    window_in(2)
    stride_on(0, zq + 3, 0, 4)
    stride_on(2, zq + 1, ROWS // 2, -4)
    window_in(3)
    arrive(jbuf.at[zq, pl.ds(0, ROWS // 2)], jr.at[1])
    arrive(jbuf.at[zq, pl.ds(0, ROWS // 2)], jr.at[3])
    for t in range(4):
        for i in range(3):
            arrive(ibuf.at[t, y], iyr.at[t, i])
            arrive(tbuf.at[t, y], tyr.at[t, i])

    over = (((1,), (1,)), ((), ()))
    own = x * 2 + core
    cols = jbuf[...].reshape(4 * ROWS, -1)
    for t in range(NX):
        part[t, 0:LANES] = lax.dot_general(
            cols, ibuf[t].reshape(NY * ROWS, -1), over, preferred_element_type=F32
        )
        low_t = tbuf[t].reshape(NY * 16, half)
        cross0 = lax.dot_general(low_t, cols[:, :half], over, preferred_element_type=F32)
        cross1 = lax.dot_general(low_t, cols[:, half:], over, preferred_element_type=F32)
        cross = cross0.reshape(NY, 16, LANES)[:, :TROWS] + cross1.reshape(NY, 16, LANES)[:, TROWS:]
        part[t, LANES:PIECE] = cross.reshape(NY * TROWS, LANES)

        @pl.when((core == 1) | (x != t))
        def _():
            send(part.at[t], rbuf.at[own], xs, xr, device(z, y, t, 0))

    def send_label(i, c):
        j = ((sup * 21) // 64 + i) % BLOCKS
        to = worker_sup(core * BLOCKS + j, x)

        @pl.when((core == 1) | (to != sup))
        def _():
            dev = {"sup": to, "cls": x * 2}
            send(labels.at[:, pl.ds(pl.multiple_of(j * LANES, LANES), LANES)], bbuf.at[sup], ls, lr, dev)
            send(cstage.at[pl.ds(0, 1)], cbuf.at[sup, pl.ds(0, 1)], cs, cr, dev)

        return c

    def send_labels():
        lax.fori_loop(0, BLOCKS, send_label, 0, unroll=3)

    @pl.when(core == 1)
    def _():
        pl.semaphore_wait(go, 1)
        send_labels()

    @pl.when(own_worker)
    def _():
        own_labels = pltpu.make_async_copy(
            labels.at[:, pl.ds(pl.multiple_of(block * LANES, LANES), LANES)], bbuf.at[sup], s7
        )
        own_labels.start()
        own_labels.wait()
        cbuf[sup] = cstage[...]

    @pl.when(core == 0)
    def _():
        gather_pieces(
            z, y, x, zq, zr, kind, zshift, send_labels, go, wide, part, rbuf, kbuf, xr, own,
            s1, r1, s2, r2, s4, r4, s5, r5, s6, r6,
        )

    def arrive_rows(t):
        for path in range(2):
            for i in range(3):
                arrive(kbuf.at[:, 0, y, :, pl.ds(0, KPART)], r4.at[path, i, t])

    lanes_at = pl.ds(pl.multiple_of(block * LANES, LANES), LANES)

    @pl.when(is_worker)
    def _():
        @pl.when(served == 0)
        def _():
            arrive(bbuf.at[pl.ds(0, NSUP - 1)], lr)
            arrive(cbuf.at[pl.ds(0, NSUP - 1), pl.ds(0, 1)], cr)

        @pl.when(served == 1)
        def _():
            arrive(bbuf, lr)
            arrive(cbuf.at[:, pl.ds(0, 1)], cr)

        def client(kk, q):
            return kk * 16 + q

        def rows_of(rho):
            return pl.ds(pl.multiple_of(rho * 512, 512), 512)

        def product(rho):
            order = [(a, b) for a in range(4) for b in range(NX)]
            rhs = jnp.concatenate(
                [pn[(a * 4 + rho + WINDOW[b] + NZ) % NZ].reshape(LANES, LANES) for a, b in order], axis=0
            )
            rows = []
            for yy in range(NY):
                for h in range(2):
                    part_rows = pl.ds(h * HALF, KPART)
                    rows.append(jnp.concatenate([kbuf[a, rho, yy, b, part_rows, :] for a, b in order], axis=1))
            return jnp.dot(jnp.concatenate(rows, axis=0), rhs, preferred_element_type=F32)

        def fold(v):
            return jnp.sum(v.reshape(64, 8, LANES), axis=0)

        def total(v):
            return jnp.sum(v, axis=0, keepdims=True)

        def to_blocks(ref, rho, v):
            v = v.reshape(NY, 4, ROWS, LANES).astype(BF16)
            for yy in range(NY):
                for kk in range(4):
                    ref[kk * 4 + rho, yy] = v[yy, kk]

        zero = jnp.zeros((8, LANES), F32)

        def solve(emit, order=None):
            def first(t, c):
                rho = t
                if order is not None:
                    rho = (z + WINDOW[t] + 4) % 4
                    arrive_rows(t)
                image = product(rho)
                b = bvec[rows_of(rho), :]
                vec[rows_of(rho), :] = image
                return c[0] + fold(b * b), c[1] + fold(b * image)

            if order is None:
                norm, curve = lax.fori_loop(0, 4, first, (zero, zero))
            else:
                norm, curve = zero, zero
                for t in order:
                    norm, curve = first(t, (norm, curve))
            norm, curve = total(norm), total(curve)
            step0 = norm / curve

            def resid(rho, c):
                v = bvec[rows_of(rho), :] - step0 * vec[rows_of(rho), :]
                vec[rows_of(rho), :] = v
                return c + fold(v * v)

            norm1 = total(lax.fori_loop(0, 4, resid, zero))
            beta = norm1 / norm

            def turn(rho, c):
                v = vec[rows_of(rho), :] + beta * bvec[rows_of(rho), :]
                vec[rows_of(rho), :] = v
                to_blocks(pn, rho, v)
                return c

            lax.fori_loop(0, 4, turn, 0)

            def second(rho, c):
                return c + fold(vec[rows_of(rho), :] * product(rho))

            step1 = norm1 / total(lax.fori_loop(0, 4, second, zero))

            def finish(i, c):
                rho = (zr + i) % 4
                emit(rho, step0 * bvec[rows_of(rho), :] + step1 * vec[rows_of(rho), :])
                return c

            lax.fori_loop(0, 4, finish, 0)

        def load(s, c):
            b = bbuf[s]
            bvec[pl.ds(pl.multiple_of(((s % 16) * 4 + s // 16) * ROWS, ROWS), ROWS), :] = b
            pn[s // 4, s % 4] = b.astype(BF16)
            return c

        lax.fori_loop(0, NSUP, load, 0)

        def keep_low(rho, v):
            low[rows_of(rho), :] = v.astype(BF16)

        solve(keep_low, range(4))

        for path in range(2):
            for i in range(3):
                arrive(kbuf.at[:, :, 0, :, pl.ds(KPART, CPART)], r5.at[path, i])

        def cross_block(q):
            rho, yy = q // 4, q % 4
            blocks = []
            for zc in range(NZ):
                b = next(i for i in range(NX) if (zc - WINDOW[i] - rho) % 4 == 0)
                zz = (zc - WINDOW[b]) % NZ
                for h in range(2):
                    blocks.append(kbuf[zz // 4, rho, yy, b, h * HALF + KPART : (h + 1) * HALF, :])
            return jnp.concatenate(blocks, axis=0)

        predicted = jnp.dot(
            jnp.concatenate([cross_block(q) for q in range(16)], axis=1), low[...], preferred_element_type=F32
        )
        pred[...] = predicted.reshape(NSUP, TROWS, LANES)

        def send_pred(i, c):
            s = (sup + i) % NSUP

            @pl.when((served == 1) | (s != sup))
            def _():
                send(pred.at[s], pbuf.at[:, lanes_at], ps, pr, {"sup": s, "cls": x * 2 + served})

            return c

        lax.fori_loop(0, NSUP, send_pred, 0, unroll=UNROLL)

        @pl.when(served == 0)
        def _():
            pbuf[:, lanes_at] = pred[sup]

        lane = lax.broadcasted_iota(jnp.int32, (NSUP, TROWS, LANES), 2)
        row = lax.broadcasted_iota(jnp.int32, (NSUP, TROWS, LANES), 1)
        target = jnp.sum(jnp.where(lane == row, cbuf[:, 0:1, :], 0.0), axis=2, keepdims=True)
        first_class = ((x * 2 + served) * BLOCKS + block) * LANES
        onehot = jnp.where(target == (first_class + lane).astype(F32), LABEL_SCALE, 0.0)
        misfit = (predicted - onehot.reshape(NSUP * TROWS, LANES)).astype(BF16)
        for q in range(16):
            rhs = lax.dot_general(cross_block(q), misfit, (((0,), (0,)), ((), ())), preferred_element_type=F32)
            bvec[q * LANES : (q + 1) * LANES, :] = rhs
            for kk in range(4):
                pn[kk * 4 + q // 4, q % 4] = rhs[kk * ROWS : (kk + 1) * ROWS].astype(BF16)

        def keep_hyper(rho, v):
            to_blocks(hst, rho, v)

        solve(keep_hyper)

        def send_hyper(i, c):
            m = i // 4
            d = jnp.where(m % 2 == 0, 8 + m // 2, 7 - m // 2)
            zz, yy = (z + d) % NZ, (y + i + 2) % 4

            @pl.when((served == 1) | (zz != z) | (yy != y))
            def _():
                dev = {"sup": zz * NY + yy, "cls": x * 2 + served}
                send(hst.at[zz, yy], hbuf.at[:, lanes_at], hs, hr, dev)

            return c

        lax.fori_loop(0, NSUP, send_hyper, 0, unroll=UNROLL)

        @pl.when(served == 0)
        def _():
            hbuf[:, lanes_at] = hst[z, y]

    @pl.when((core == 0) & (kind < 3) & jnp.logical_not(is_worker))
    def _():
        for t in range(4):
            arrive_rows(t)
        for path in range(2):
            for i in range(3):
                arrive(kbuf.at[:, :, 0, :, pl.ds(KPART, CPART)], r5.at[path, i])

    def settle(buf, axis, sem, count):
        full, less = [slice(None)] * buf.ndim, [slice(None)] * buf.ndim
        less[axis] = pl.ds(0, (count - 1) * (buf.shape[axis] // count))

        @pl.when(own_worker)
        def _():
            arrive(buf.at[tuple(less)], sem)

        @pl.when(others)
        def _():
            arrive(buf.at[tuple(full)], sem)

    for t in range(3):
        arrive(ibuf.at[0, y], iws.at[t])
        arrive(tbuf.at[0, y], tws.at[t])
        for k in range(4):
            arrive(ibuf.at[0, y], iys.at[k, t])
            arrive(tbuf.at[0, y], tys.at[k, t])
    for i in range(2):
        arrive(jbuf.at[zq], js.at[2 * i])
        arrive(jbuf.at[zq, pl.ds(0, ROWS // 2)], js.at[2 * i + 1])
    settle(labels, 1, ls, BLOCKS)

    @pl.when(own_worker)
    def _():
        arrive(cbuf.at[pl.ds(0, BLOCKS - 1), pl.ds(0, 1)], cs)

    @pl.when(others)
    def _():
        arrive(cbuf.at[pl.ds(0, BLOCKS), pl.ds(0, 1)], cs)

    @pl.when(core == 0)
    def _():
        arrive(part.at[pl.ds(0, NX - 1)], xs)
        arrive(kbuf.at[0, 0, 0, pl.ds(0, 3)], s1)
        arrive(kbuf.at[:, 0, 0, pl.ds(0, 3)], s6)
        for path in range(2):
            arrive(kbuf.at[:, 0, pl.ds(0, 3), :, pl.ds(0, HALF)], s2.at[path])

            def sent(count):
                arrive(kbuf.at[:, :, pl.ds(0, count), :, pl.ds(0, KPART)], s4.at[path])
                arrive(kbuf.at[:, :, pl.ds(0, count), :, pl.ds(KPART, CPART)], s5.at[path])

            pl.when(kind < 3)(functools.partial(sent, 2))
            pl.when(kind == 3)(functools.partial(sent, 3))

    @pl.when(core == 1)
    def _():
        arrive(part, xs)

    @pl.when(is_worker & (served == 0))
    def _():
        arrive(pred.at[pl.ds(0, NSUP - 1)], ps)
        arrive(low.at[pl.ds(0, (NSUP - 1) * ROWS)], hs)

    @pl.when(is_worker & (served == 1))
    def _():
        arrive(pred, ps)
        arrive(low, hs)

    settle(pbuf, 1, pr, BLOCKS)
    settle(hbuf, 1, hr, BLOCKS)


def gather_pieces(
    z, y, x, zq, zr, kind, zshift, send_labels, go, scales, part, rbuf, kbuf, xr, own,
    s1, r1, s2, r2, s4, r4, s5, r5, s6, r6,
):
    rbuf[own] = part[x]
    arrive(rbuf.at[pl.ds(0, 2 * NX - 1)], xr)
    summed = rbuf[0]
    for k in range(1, 2 * NX):
        summed = summed + rbuf[k]
    zc = zshift(jnp.where(x < 2, x, jnp.where(x == 2, WINDOW[2], WINDOW[3])))
    col_scale = scales[pl.ds(zc, 1), :]
    lane = lax.broadcasted_iota(jnp.int32, (ROWS, LANES), 1)
    row = lax.broadcasted_iota(jnp.int32, (ROWS, LANES), 0)
    row_scales = []
    for kk in range(4):
        zz = kk * 4 + zr
        picked = jnp.where(lane == y * ROWS + row, scales[pl.ds(zz, 1), :], 0.0)
        row_scale = jnp.sum(picked, axis=1, keepdims=True)
        row_scales.append(row_scale)
        diag = zz * LANES + y * ROWS + row == zc * LANES + lane
        block = summed[kk * ROWS : (kk + 1) * ROWS] * (row_scale * col_scale) / F
        at = (kk // 2) * HALF + (kk % 2) * ROWS
        kbuf[zq, zr, y, x, at : at + ROWS] = (block + jnp.where(diag, RIDGE, 0.0)).astype(BF16)
    row_scale = jnp.concatenate(row_scales, axis=0)
    same = lax.broadcasted_iota(jnp.int32, (LANES, LANES), 0) == lax.broadcasted_iota(jnp.int32, (LANES, LANES), 1)
    cross_scale = jnp.sum(jnp.where(same, row_scale, 0.0), axis=0, keepdims=True)
    for h in range(2):
        cross = summed[LANES + h * CPART : LANES + (h + 1) * CPART] * cross_scale / F
        kbuf[zq, zr, y, x, h * HALF + KPART : (h + 1) * HALF] = cross.astype(BF16)

    pos = (y, x)

    def last_dev(path, k):
        if path == 0:
            return device(z, (y + k) % NY, x, 0)
        return device(z, y, (x + k) % NX, 0)

    def line(path, k):
        if path == 0:
            return device(z, y, (x + k) % NX, 0)
        return device(z, (y + k) % NY, x, 0)

    def rho_of(t):
        return (z + WINDOW[t] + 4) % 4

    def window_send(ref, send_sem, recv_sems, ts):
        for t in ts:
            send(ref, ref, send_sem, recv_sems.at[t - 1], device(zshift(-WINDOW[t]), y, x, 0))

    piece = kbuf.at[zq, zr, y, x]
    for i in (2, 1, 3):
        send(piece, piece, s1, r1.at[i - 1], device(zshift(4 * i), y, x, 0))
    window_send(piece, s6, r6, (1, 2, 3))
    for i in (1, 3, 2):
        arrive(piece, r1.at[i - 1])
        window_send(kbuf.at[(zq + 4 - i) % 4, zr, y, x], s6, r6, (1, 2, 3))
    def middle(t):
        for i in (1, 3, 2):
            for path in range(2):
                ref = kbuf.at[:, rho_of(t), y, x, pl.ds(path * HALF, HALF)]
                send(ref, ref, s2.at[path], r2.at[path, i - 1, t], line(path, i))

    for t in range(4):
        if t > 0:
            arrive(kbuf.at[:, 0, y, x], r6.at[t - 1])
        middle(t)
        if t == LABELS_AFTER:
            signal(go, device(z, y, x, 1))
            send_labels()

    def last(t):
        rho = rho_of(t)
        for a in range(4 // SPLIT):
            refs = (
                kbuf.at[pl.ds(SPLIT * a, SPLIT), rho, y, :, pl.ds(0, KPART)],
                kbuf.at[pl.ds(SPLIT * a, SPLIT), rho, :, x, pl.ds(HALF, KPART)],
            )
            for i in (1, 3, 2):

                @pl.when((kind + i) % 4 < 3)
                def _():
                    for path in range(2):
                        send(refs[path], refs[path], s4.at[path], r4.at[path, i - 1, t], last_dev(path, i))

    for t in range(4):
        for path in range(2):
            for i in range(3):
                arrive(kbuf.at[:, 0, y, x, pl.ds(0, HALF)], r2.at[path, i, t])
        last(t)
    refs = (kbuf.at[:, :, y, :, pl.ds(KPART, CPART)], kbuf.at[:, :, :, x, pl.ds(HALF + KPART, CPART)])
    for i in (1, 3, 2):

        @pl.when((kind + i) % 4 < 3)
        def _():
            for path in range(2):
                send(refs[path], refs[path], s5.at[path], r5.at[path, i - 1], last_dev(path, i))


def local(support_feats, target_feats, scales, soft_labels, target_labels):
    width = support_feats.shape[1]
    dma = pltpu.SemaphoreType.DMA
    vmem = pl.BlockSpec(memory_space=pltpu.VMEM)
    pred, hyper = pl.pallas_call(
        kernel,
        out_shape=(
            jax.ShapeDtypeStruct((TROWS, BLOCKS * LANES), F32),
            jax.ShapeDtypeStruct((ROWS, BLOCKS * LANES), BF16),
        ),
        in_specs=[pl.BlockSpec(memory_space=pl.ANY), vmem, vmem, pl.BlockSpec(memory_space=pl.ANY), pl.BlockSpec(memory_space=pltpu.SMEM)],
        out_specs=(vmem, vmem),
        scratch_shapes=[
            pltpu.VMEM((4, NY, ROWS, width), BF16),
            pltpu.VMEM((4, NY, 16, width // 2), BF16),
            pltpu.VMEM((4, ROWS, width), BF16),
            pltpu.VMEM((NX, PIECE, LANES), F32),
            pltpu.VMEM((2 * NX, PIECE, LANES), F32),
            pltpu.VMEM((4, 4, NY, NX, PIECE, LANES), BF16),
            pltpu.VMEM((8, LANES), F32),
            pltpu.VMEM((NSUP, 8, LANES), F32),
            pltpu.VMEM((NSUP, ROWS, LANES), F32),
            pltpu.VMEM((NZ, NY, ROWS, LANES), BF16),
            pltpu.VMEM((2048, LANES), F32),
            pltpu.VMEM((2048, LANES), F32),
            pltpu.VMEM((2048, LANES), BF16),
            pltpu.VMEM((NSUP, TROWS, LANES), F32),
            pltpu.VMEM((NZ, NY, ROWS, LANES), BF16),
            pltpu.VMEM((NZ, LANES), F32),
            pltpu.SemaphoreType.REGULAR,
            dma((3,)), dma((3,)), dma((3,)), dma((3,)),
            dma((4, 3)), dma((4, 3)), dma((4, 3)), dma((4, 3)),
            dma((4,)), dma((4,)), dma, dma,
            dma, dma, dma, dma,
            dma, dma((3,)), dma((2,)), dma((2, 3, 4)),
            dma((2,)), dma((2, 3, 4)), dma((2,)), dma((2, 3)), dma, dma((3,)), dma,
            dma, dma, dma, dma,
        ],
        compiler_params=pltpu.CompilerParams(collective_id=0, has_side_effects=True, vmem_limit_bytes=56 * 2**20),
        name="hypergradient",
    )(support_feats, target_feats, scales.reshape(NZ, LANES), soft_labels, target_labels)
    return pred.astype(BF16), hyper.astype(F32)


def solution(mesh):
    in_specs = (P("sup", "cls"), P("sup", "cls"), P(), P("sup", "cls"), P("sup"))
    out_specs = (P("sup", "cls"), P("sup", "cls"))
    return jax.shard_map(local, mesh=mesh, in_specs=in_specs, out_specs=out_specs, check_vma=False)
```
